256 devices in a mesh: phase: 8 (over z), dp: 2 (over y_lo), mp: 16 (over y_hi, x, core).
Axes of the slice: x: 4, y: 4 (y_hi: 2, y_lo: 2; y = y_hi * 2 + y_lo), z: 8, core: 2. Of those that a mesh axis runs over, the one named last changes fastest.
Arguments:
- text_embeds: bfloat16 [16, 2048, 8192], P(('phase', 'dp'), None, 'mp'), may hold values from -6 to 6
- image_tokens: bfloat16 [16, 768, 8192], P(('phase', 'dp'), 'mp'), may hold values from -8 to 8
- image_slots: int32 [16, 768], P(('phase', 'dp'), 'mp'), may hold values from 0 to 2047, as said below
- segment_ids: int32 [16, 2048], P(('phase', 'dp')), may hold values from 0 to 7, never falling along the last dimension, each value on 1 to 512 neighbouring positions
- norm_gain: float32 [8192], P('mp'), may hold values from 0.1 to 1.9
- kv_weight: bfloat16 [8192, 2048], P('mp'), may hold values from -0.0625 to 0.0625
- kv_bias: float32 [2048], replicated, may hold values from -3 to 3
- kv_cotangent: bfloat16 [16, 2048, 2048], P(('phase', 'dp'), 'mp'), may hold values from -6 to 6
Outputs:
- kv_states: bfloat16 [16, 2048, 2048], P(('phase', 'dp'), 'mp')
- text_grad: bfloat16 [16, 2048, 8192], P(('phase', 'dp'), None, 'mp')
- image_grad: bfloat16 [16, 768, 8192], P(('phase', 'dp'), 'mp')
- weight_grad: float32 [8192, 2048], P('mp', ('phase', 'dp'))
- bias_grad: float32 [2048], P(('phase', 'dp'))
- gain_grad: float32 [8192], P('mp')
The draws below stay inside these ranges and needn't reach their ends.
Inputs may be any that keep to these rules, and one draw needn't show every extreme that they name: `image_slots`: in each sequence the 768 positions are distinct, and both 0 and 2047 occur.
All inputs are finite; a program needn't handle non-finite values.
Results may differ from the reference program's by a relative error of at most 0.018.
Values may be sent and summed in bfloat16 or wider, within the bound.
No kernel may reach another device: no remote copies, remote signals or barrier semaphores. Data moves between devices by JAX's collectives and lax.ppermute only.
A program may use at most 128 MiB of HBM per device.

```python
import math
import jax
import jax.numpy as jnp
import numpy as np
from jax import lax

D = 8192
KV_HEADS = 8
HEAD = 128
DOCS = 8
SEQ = 2048
SEQS = 16
IMGS = 768
KV = 2048
N_MP = 16


def draw_image_slots(key, part):
    key = jax.random.fold_in(key, 11)

    def single_row(row_key):
        inner_pick = jax.random.permutation(row_key, SEQ - 2).astype(jnp.int32) + 1
        chosen = jnp.concatenate([jnp.zeros((1,), jnp.int32), jnp.full((1,), SEQ - 1, jnp.int32), inner_pick[:IMGS - 2]])
        return jax.random.permutation(jax.random.fold_in(row_key, 1), chosen).astype(jnp.int32)
    row_keys = jax.random.split(key, SEQS)
    return jax.vmap(single_row)(row_keys).astype(jnp.int32)


def raised(array, own_key, source, target, shards_of, factor):
    owner, partner = [(jnp.arange(array.shape[axis_at]) // (array.shape[axis_at] // shards_of)).reshape([-1 if axis == axis_at else 1 for axis in range(array.ndim)]) for axis_at in (source, target)]
    chosen = jax.random.permutation(own_key, shards_of)[partner]
    strong = (owner == chosen) | (owner == (partner + shards_of // 2) % shards_of)
    return jnp.where(strong, factor * array, array)


def steps_of(own_key, extent, cuts, smallest, high):
    def one(dim, blocks):
        heights = jax.random.uniform(jax.random.fold_in(jax.random.fold_in(own_key, 6), dim), (blocks,), jnp.float32, smallest / len(cuts), high / len(cuts))
        return jnp.repeat(jnp.exp(heights), extent[dim] // blocks).reshape((-1,) + (1,) * (len(extent) - dim - 1))

    factor_of = one(*cuts[0])
    for cut in cuts[1:]:
        factor_of = factor_of * one(*cut)
    return factor_of


def length_profile(amount, total, limit, skew):
    portions = [(1 << 20) // math.isqrt(standing ** skew) + 1 for standing in range(2, amount + 1)]
    surplus, given = total - limit - (amount - 1), [1] * (amount - 1)
    while surplus > 0:
        movable = [i for i in range(amount - 1) if given[i] < limit]
        whole, left = sum([portions[i] for i in movable]), surplus
        for i in movable:
            addition = min(limit - given[i], max(1, left * portions[i] // whole), surplus)
            given[i] = given[i] + addition
            surplus = surplus - addition
    return np.array([limit] + given)


def ragged(key, count, total, bound, skew):
    if count == 2:
        one = jax.random.randint(key, (), max(1, total - bound), min(bound, total - 1) + 1)
        return jnp.stack([one, total - one])
    lengths = jnp.asarray(length_profile(count, total, bound, skew), jnp.int32)
    couples = (count - 1) // 2
    giver, sink = lengths[1:1 + 2 * couples:2], lengths[2:2 + 2 * couples:2]
    slack = jnp.minimum(giver - 1, bound - sink)
    passed = jax.random.randint(jax.random.fold_in(key, 1), (couples,), 0, 1 << 20) % (slack + 1)
    lengths = lengths.at[1:1 + 2 * couples:2].set(giver - passed).at[2:2 + 2 * couples:2].set(sink + passed)
    return lengths[jax.random.permutation(jax.random.fold_in(key, 2), count)]


def normal_values(key, dims, width, reach, shards=(), kind=jnp.bfloat16):
    level = steps_of(key, dims, shards, -0.22, 0.18) if shards else 1.0
    result = jax.random.normal(key, dims, jnp.float32) * width * level
    return jnp.minimum(jnp.maximum(result, -reach), reach).astype(kind)


def noise_with(key, extent, spread, reach, pieces, heavy, kind=jnp.bfloat16):
    result = spread * jax.random.normal(key, extent, jnp.float32)
    if pieces:
        result = result * steps_of(key, extent, pieces, -0.22, 0.18)
    return jnp.clip(raised(result, jax.random.fold_in(key, 3), *heavy), -reach, reach).astype(kind)


def setup_inputs(seed: int = 0) -> dict:
    keys = jax.random.split(jax.random.key(seed), 9)
    return {
        "text_embeds": normal_values(keys[0], (SEQS, SEQ, D), 1.0, 6.0, ((0, 16), (2, 16))),
        "image_tokens": normal_values(keys[1], (SEQS, IMGS, D), 1.5, 8.0, ((0, 16), (1, 16))),
        "image_slots": draw_image_slots(jax.random.fold_in(keys[8], 71), 0),
        "segment_ids": jax.vmap(lambda own: jnp.searchsorted(jnp.cumsum(ragged(own, DOCS, SEQ, SEQ // 4, 2)), jnp.arange(SEQ), side="right"))(jax.random.split(keys[3], SEQS)).reshape((SEQS, SEQ)).astype(jnp.int32),
        "norm_gain": jnp.clip(1.0 + 0.18 * jax.random.normal(keys[4], (D,), jnp.float32), 0.1, 1.9),
        "kv_weight": normal_values(keys[5], (D, KV), D ** -0.5, 0.0625, ((0, 16),)),
        "kv_bias": normal_values(keys[6], (KV,), 0.5, 3.0, (), jnp.float32),
        "kv_cotangent": noise_with(keys[7], (SEQS, SEQ, KV), 1.0, 6.0, ((0, 16), (1, 16)), (0, 2, 16, 2.0)),
    }


epsilon_value = 1e-06
rope_base = 1000000.0

def rotate(values, positions, direction):
    row_total = values.shape[0]
    half_head = HEAD // 2
    frequency = rope_base ** (-(jnp.arange(half_head, dtype=jnp.float32) * 2.0) / HEAD)
    angles = positions.astype(jnp.float32)[:, None] * frequency[None, :]
    cosine = jnp.cos(angles)[:, None, :]
    sine_part = direction * jnp.sin(angles)[:, None, :]
    shaped = values.reshape(row_total, -1, HEAD)
    first_half = shaped[..., :half_head]
    second_half = shaped[..., half_head:]
    rotated_rows = jnp.concatenate([first_half * cosine - second_half * sine_part, second_half * cosine + first_half * sine_part], axis=-1)
    return rotated_rows.reshape(row_total, -1)

def rotate_keys(values, positions, direction):
    key_width = KV_HEADS * HEAD
    return jnp.concatenate([rotate(values[:, :key_width], positions, direction), values[:, key_width:]], axis=1)

def document_positions(segment):
    length_total = segment.shape[0]
    row_index = jnp.arange(length_total, dtype=jnp.int32)
    previous = jnp.concatenate([segment[:1] - 1, segment[:-1]])
    starts = lax.cummax(jnp.where(segment != previous, row_index, 0), axis=0)
    return row_index - starts

def reference(text_embeds, image_tokens, image_slots, segment_ids, norm_gain, kv_weight, kv_bias, kv_cotangent):
    block_width = D // N_MP

    def per_sequence(running, inputs):
        text_rows, image_rows, slot_list, segment, cotangent = inputs
        hidden = text_rows.at[slot_list].set(image_rows)
        hidden_wide = hidden.astype(jnp.float32)
        inverse_rms = lax.rsqrt(lax.optimization_barrier(jnp.sum(hidden_wide * hidden_wide, axis=-1)) / D + epsilon_value)
        normed = (hidden_wide * inverse_rms[:, None] * norm_gain[None, :]).astype(jnp.bfloat16)
        running_sum = jnp.zeros((SEQ, KV), jnp.float32)
        for block_index in range(N_MP):
            lower = block_index * block_width
            block_term = jnp.dot(normed[:, lower:lower + block_width], kv_weight[lower:lower + block_width], preferred_element_type=jnp.float32)
            rounded = lax.optimization_barrier(block_term.astype(jnp.bfloat16))
            running_sum = running_sum + rounded.astype(jnp.float32)
        positions = document_positions(segment)
        states = rotate_keys(running_sum + kv_bias[None, :], positions, 1.0).astype(jnp.bfloat16)
        back_states = rotate_keys(cotangent.astype(jnp.float32), positions, -1.0).astype(jnp.bfloat16)
        grad_normed = jnp.dot(back_states, kv_weight.T, preferred_element_type=jnp.float32)
        grad_weight = jnp.dot(normed.T, back_states, preferred_element_type=jnp.float32)
        grad_bias = lax.optimization_barrier(jnp.sum(back_states.astype(jnp.float32), axis=0))
        grad_gain = lax.optimization_barrier(jnp.sum(grad_normed * hidden_wide * inverse_rms[:, None], axis=0))
        inner_sum = lax.optimization_barrier(jnp.sum(grad_normed * norm_gain[None, :] * hidden_wide, axis=-1))
        grad_hidden = inverse_rms[:, None] * norm_gain[None, :] * grad_normed - hidden_wide * (inverse_rms ** 3 * inner_sum / D)[:, None]
        image_mask = jnp.zeros((SEQ,), jnp.bool_).at[slot_list].set(True)
        grad_text = jnp.where(image_mask[:, None], 0.0, grad_hidden).astype(jnp.bfloat16)
        grad_image = grad_hidden[slot_list].astype(jnp.bfloat16)
        running = (running[0] + grad_weight, running[1] + grad_bias, running[2] + grad_gain)
        return (running, (states, grad_text, grad_image))
    initial = (jnp.zeros((D, KV), jnp.float32), jnp.zeros((KV,), jnp.float32), jnp.zeros((D,), jnp.float32))
    totals, outputs = lax.scan(per_sequence, initial, (text_embeds, image_tokens, image_slots, segment_ids, kv_cotangent))
    return (outputs[0], outputs[1], outputs[2], totals[0], totals[1], totals[2])
```

```python
import jax
import jax.numpy as jnp
from jax import lax
from jax.experimental import pallas as pl
from jax.experimental.pallas import tpu as pltpu
from jax.sharding import PartitionSpec as P

D = 8192
HEAD = 128
epsilon_value = 1e-06
rope_base = 1000000.0

BF = jnp.bfloat16
F32 = jnp.float32

ORDER = ((1, 1), (1, 3), (1, 2), (0, 2), (1, 0), (0, 1), (0, 3), (0, 0))
PLACE = {chip: index for index, chip in enumerate(ORDER)}
MIB = 1 << 20


def take(value, dy, dx, dc=0):
    pairs = []
    for y in range(2):
        for x in range(4):
            for c in range(2):
                source = (((y + dy) % 2) * 4 + (x + dx) % 4) * 2 + (c + dc) % 2
                pairs.append((source, (y * 4 + x) * 2 + c))
    return lax.ppermute(value, "mp", pairs)


def take_mirror(value):
    pairs = []
    for y in range(2):
        for x in range(4):
            for c in range(2):
                pairs.append(((y * 4 + 3 - x) * 2 + c, (y * 4 + x) * 2 + c))
    return lax.ppermute(value, "mp", pairs)


def take_swap(value):
    pairs = []
    for y in range(2):
        for x in range(4):
            for c in range(2):
                pairs.append(((y * 4 + (x ^ 1)) * 2 + c, (y * 4 + x) * 2 + c))
    return lax.ppermute(value, "mp", pairs)


def take_phase(value, dz):
    return lax.ppermute(value, "phase", [((p + dz) % 8, p) for p in range(8)])


def take_phase_xor(value, bit):
    return lax.ppermute(value, "phase", [(p ^ bit, p) for p in range(8)])


def take_dp(value):
    return lax.ppermute(value, "dp", [(0, 1), (1, 0)])


def chip_sum(value):
    value = value + take_swap(value)
    value = value + take_mirror(value)
    return value + take(value, 1, 0)


def add(*values):
    total = values[0].astype(F32)
    for value in values[1:]:
        total = total + value.astype(F32)
    return total


def gather_rows(block):
    half = block.shape[0] // 2
    r = {(0, 0): block}
    r[0, 1] = take(block, 0, 1)
    r[0, 3] = take(block, 0, 3)
    r[1, 0] = take(block, 1, 0)
    low = take(r[0, 1][:half], 0, 1)
    high = take(r[0, 3][half:], 0, 3)
    r[1, 1] = take(r[1, 0], 0, 1)
    r[1, 3] = take(r[1, 0], 0, 3)
    far_low = take(low, 1, 0)
    far_high = take(high, 1, 0)
    parts = []
    for chip in ORDER:
        if chip == (0, 2):
            parts += [low, high]
        elif chip == (1, 2):
            parts += [far_low, far_high]
        else:
            parts.append(r[chip])
    return jnp.concatenate(parts, axis=0)


def reduce_rows(terms):
    rows = terms.shape[0] // 8
    half = rows // 2
    q = {chip: terms[i * rows : (i + 1) * rows] for chip, i in PLACE.items()}
    left = take(q[1, 1], 0, 3)
    right = take(q[1, 3], 0, 1)
    across = take(q[1, 2], 1, 0)
    far = add(q[0, 2], across).astype(BF)
    up = take(far[:half], 0, 3)
    down = take(far[half:], 0, 1)
    partner = add(q[1, 0], left, right).astype(BF)
    over = take(partner, 1, 0)
    forth = jnp.concatenate([add(q[0, 1][:half], up).astype(BF), q[0, 1][half:]], axis=0)
    back = jnp.concatenate([q[0, 3][:half], add(q[0, 3][half:], down).astype(BF)], axis=0)
    return add(q[0, 0], take(forth, 0, 3), take(back, 0, 1), over)


def phase_reduce(blocks):
    rows = blocks[0].shape[0]
    half = 256
    b = list(blocks)
    up = take_phase(b[4][:half], -1)
    down = take_phase(b[4][half:], 1)
    b[3] = jnp.concatenate([add(b[3][:half], up).astype(BF), b[3][half:]], axis=0)
    b[5] = jnp.concatenate([b[5][:half], add(b[5][half:], down).astype(BF)], axis=0)
    b[2] = add(b[2], take_phase(b[3], -1)).astype(BF)
    b[6] = add(b[6], take_phase(b[5], 1)).astype(BF)
    b[1] = add(b[1], take_phase(b[2], -1)).astype(BF)
    b[7] = add(b[7], take_phase(b[6], 1)).astype(BF)
    return add(b[0], take_phase(b[1], -1), take_phase(b[7], 1))


def rotate(half_columns, cosine, sine):
    rows = half_columns.shape[0]
    width = half_columns.shape[1] // 2
    heads = half_columns[:, :width].reshape(rows, -1, HEAD)
    swapped = jnp.concatenate([heads[..., HEAD // 2 :], heads[..., : HEAD // 2]], axis=-1)
    turned = heads * cosine[:, None, :] + swapped * sine[:, None, :]
    return jnp.concatenate([turned.reshape(rows, width), half_columns[:, width:]], axis=1)


def hidden_kernel(place, slots, images, text, own, other):
    j = pl.program_id(0)
    count = slots.shape[1]
    rows = text.shape[0]
    half = rows // 2
    token = place[j] * rows + lax.broadcasted_iota(jnp.int32, (rows, count), 0)
    hit = (token == slots[...]).astype(F32)
    picked = jnp.dot(hit.astype(BF), images[...], preferred_element_type=F32)
    named = jnp.max(hit, axis=1, keepdims=True) > 0.5
    hidden = jnp.where(named, picked, text[...].astype(F32)).astype(BF)
    core = place[8]

    @pl.when(core == 0)
    def _():
        own[...] = hidden[:half]
        other[...] = hidden[half:]

    @pl.when(core != 0)
    def _():
        own[...] = hidden[half:]
        other[...] = hidden[:half]


def build_hidden(place, slots, images, text):
    rows, width = text.shape
    block = rows // 8
    half = block // 2
    return pl.pallas_call(
        hidden_kernel,
        grid_spec=pltpu.PrefetchScalarGridSpec(
            num_scalar_prefetch=1,
            grid=(8,),
            in_specs=[
                pl.BlockSpec(slots.shape, lambda j, place: (0, 0)),
                pl.BlockSpec(images.shape, lambda j, place: (0, 0)),
                pl.BlockSpec((block, width), lambda j, place: (place[j], 0)),
            ],
            out_specs=[
                pl.BlockSpec((half, width), lambda j, place: (j, 0)),
                pl.BlockSpec((half, width), lambda j, place: (j, 0)),
            ],
        ),
        out_shape=[jax.ShapeDtypeStruct((rows // 2, width), BF)] * 2,
        compiler_params=pltpu.CompilerParams(vmem_limit_bytes=24 * MIB),
        cost_estimate=pl.CostEstimate(
            flops=2 * rows * width * images.shape[0], bytes_accessed=6 * MIB, transcendentals=0
        ),
        name="build_hidden",
    )(place, slots, images, text)


def project_kernel(own, met, gain_own, gain_met, weight_own, weight_met, out):
    a = (own[...].astype(F32) * gain_own[...]).astype(BF)
    b = (met[...].astype(F32) * gain_met[...]).astype(BF)
    out[...] = (
        jnp.dot(a, weight_own[...], preferred_element_type=F32)
        + jnp.dot(b, weight_met[...], preferred_element_type=F32)
    ).astype(BF)


def project(own, met, gain_own, gain_met, weight_own, weight_met, part):
    rows, width = own.shape
    block = rows // 4
    columns = weight_own.shape[1] // 2
    return pl.pallas_call(
        project_kernel,
        grid=(4,),
        in_specs=[
            pl.BlockSpec((block, width), lambda i: (i, 0)),
            pl.BlockSpec((block, width), lambda i: (i, 0)),
            pl.BlockSpec((1, width), lambda i: (0, 0)),
            pl.BlockSpec((1, width), lambda i: (0, 0)),
            pl.BlockSpec((width, columns), lambda i: (0, part)),
            pl.BlockSpec((width, columns), lambda i: (0, part)),
        ],
        out_specs=pl.BlockSpec((block, columns), lambda i: (i, 0)),
        out_shape=jax.ShapeDtypeStruct((rows, columns), BF),
        compiler_params=pltpu.CompilerParams(vmem_limit_bytes=32 * MIB),
        cost_estimate=pl.CostEstimate(
            flops=4 * rows * width * columns, bytes_accessed=6 * MIB, transcendentals=0
        ),
        name="project",
    )(own, met, gain_own, gain_met, weight_own, weight_met)


def weight_grad_kernel(place, own, met, gain_own, gain_met, scale, back, out_own, out_met, total):
    width = own.shape[1]
    columns = back.shape[1]
    phase = place[9]
    value = back[...]
    bias = jnp.sum(value.astype(F32), axis=0, keepdims=True)
    first = lax.broadcasted_iota(jnp.int32, (16, columns), 0) == 0
    total[width:, :] = jnp.where(first, bias, 0.0).astype(BF)
    for source, gain, out in ((own, gain_own, out_own), (met, gain_met, out_met)):
        normed = (source[...].astype(F32) * scale[...] * gain[...]).astype(BF)
        total[:width, :] = lax.dot_general(
            normed, value, (((0,), (0,)), ((), ())), preferred_element_type=F32
        ).astype(BF)
        for j in range(8):
            start = pl.multiple_of(lax.rem(phase + j, 8) * HEAD, HEAD)
            out[:, j * HEAD : (j + 1) * HEAD] = total[:, pl.ds(start, HEAD)]


def weight_grad(place, own, met, gain_own, gain_met, scale, back):
    rows, width = own.shape
    columns = back.shape[1]
    whole = pl.BlockSpec(memory_space=pltpu.VMEM)
    return pl.pallas_call(
        weight_grad_kernel,
        in_specs=[pl.BlockSpec(memory_space=pltpu.SMEM)] + [whole] * 6,
        out_specs=[whole] * 2,
        out_shape=[jax.ShapeDtypeStruct((width + 16, columns), BF)] * 2,
        scratch_shapes=[pltpu.VMEM((width + 16, columns), BF)],
        compiler_params=pltpu.CompilerParams(vmem_limit_bytes=40 * MIB),
        cost_estimate=pl.CostEstimate(
            flops=4 * rows * width * columns, bytes_accessed=6 * MIB, transcendentals=0
        ),
        name="weight_grad",
    )(place, own, met, gain_own, gain_met, scale, back)


def hidden_grad_kernel(
    back_a, back_b, own, met, gain_own, gain_met, weight_own, weight_met, scale, pull,
    grad_own, grad_met, sum_own, sum_met,
):
    columns = back_a.shape[1]
    last = (((1,), (1,)), ((), ()))
    a, b, s, q = back_a[...], back_b[...], scale[...], pull[...]
    for source, gain, weight, grad, total in (
        (own, gain_own, weight_own, grad_own, sum_own),
        (met, gain_met, weight_met, grad_met, sum_met),
    ):
        normed_grad = lax.dot_general(
            a, weight[:, :columns], last, preferred_element_type=F32
        ) + lax.dot_general(b, weight[:, columns:], last, preferred_element_type=F32)
        hidden = source[...].astype(F32)
        scaled = normed_grad * s
        grad[...] = (scaled * gain[...] - hidden * q).astype(BF)
        part = jnp.sum(scaled * hidden, axis=0, keepdims=True)

        @pl.when(pl.program_id(0) == 0)
        def _():
            total[...] = part

        @pl.when(pl.program_id(0) != 0)
        def _():
            total[...] += part


def hidden_grad(back_a, back_b, own, met, gain_own, gain_met, weight_own, weight_met, scale, pull):
    rows, width = own.shape
    block = rows // 4
    columns = back_a.shape[1]
    tall = pl.BlockSpec((block, width), lambda i: (i, 0))
    wide = pl.BlockSpec((block, columns), lambda i: (i, 0))
    thin = pl.BlockSpec((block, 1), lambda i: (i, 0))
    line = pl.BlockSpec((1, width), lambda i: (0, 0))
    matrix = pl.BlockSpec(weight_own.shape, lambda i: (0, 0))
    return pl.pallas_call(
        hidden_grad_kernel,
        grid=(4,),
        in_specs=[wide, wide, tall, tall, line, line, matrix, matrix, thin, thin],
        out_specs=[tall, tall, line, line],
        out_shape=[jax.ShapeDtypeStruct((rows, width), BF)] * 2
        + [jax.ShapeDtypeStruct((1, width), F32)] * 2,
        compiler_params=pltpu.CompilerParams(vmem_limit_bytes=40 * MIB),
        cost_estimate=pl.CostEstimate(
            flops=8 * rows * width * columns, bytes_accessed=14 * MIB, transcendentals=0
        ),
        name="hidden_grad",
    )(back_a, back_b, own, met, gain_own, gain_met, weight_own, weight_met, scale, pull)


def split_kernel(place, slots, slot_lines, own, met, text, images, total):
    j = pl.program_id(0)
    core = place[8]
    count = slots.shape[1]
    half = own.shape[0]
    rows = 2 * half
    base = place[j] * rows
    one, two = own[...], met[...]
    value = jnp.concatenate(
        [
            jnp.where(core == 0, one.astype(F32), two.astype(F32)),
            jnp.where(core == 0, two.astype(F32), one.astype(F32)),
        ],
        axis=0,
    )
    hit = (base + lax.broadcasted_iota(jnp.int32, (rows, count), 0) == slots[...]).astype(F32)
    named = jnp.max(hit, axis=1, keepdims=True) > 0.5
    text[...] = jnp.where(named, 0.0, value).astype(BF)
    pick = (base + lax.broadcasted_iota(jnp.int32, (count, rows), 1) == slot_lines[...]).astype(F32)
    part = jnp.dot(pick.astype(BF), value.astype(BF), preferred_element_type=F32)

    @pl.when(j == 0)
    def _():
        total[...] = part

    @pl.when(j != 0)
    def _():
        total[...] += part

    @pl.when(j == 7)
    def _():
        images[...] = total[...].astype(BF)


def split_grads(place, slots, own, met):
    rows, width = own.shape
    half = rows // 8
    count = slots.shape[1]
    return pl.pallas_call(
        split_kernel,
        grid_spec=pltpu.PrefetchScalarGridSpec(
            num_scalar_prefetch=1,
            grid=(8,),
            in_specs=[
                pl.BlockSpec((1, count), lambda j, place: (0, 0)),
                pl.BlockSpec((count, 1), lambda j, place: (0, 0)),
                pl.BlockSpec((half, width), lambda j, place: (j, 0)),
                pl.BlockSpec((half, width), lambda j, place: (j, 0)),
            ],
            out_specs=[
                pl.BlockSpec((2 * half, width), lambda j, place: (place[j], 0)),
                pl.BlockSpec((count, width), lambda j, place: (0, 0)),
            ],
            scratch_shapes=[pltpu.VMEM((count, width), F32)],
        ),
        out_shape=[
            jax.ShapeDtypeStruct((2 * rows, width), BF),
            jax.ShapeDtypeStruct((count, width), BF),
        ],
        compiler_params=pltpu.CompilerParams(vmem_limit_bytes=24 * MIB),
        cost_estimate=pl.CostEstimate(
            flops=4 * rows * width * count, bytes_accessed=6 * MIB, transcendentals=0
        ),
        name="split_grads",
    )(place, slots, slots.reshape(count, 1), own, met)


def per_device(
    text_embeds, image_tokens, image_slots, segment_ids, norm_gain, kv_weight, kv_bias, kv_cotangent
):
    mp_index = lax.axis_index("mp")
    phase = lax.axis_index("phase")
    dp = lax.axis_index("dp")
    core = mp_index % 2
    column = (mp_index // 2) % 4
    row = mp_index // 8
    chips = jnp.stack([((row + dy) % 2) * 4 + (column + dx) % 4 for dy, dx in ORDER])
    place = jnp.concatenate([chips, core[None], phase[None]]).astype(jnp.int32)

    own_rows = kv_cotangent.shape[1]
    segment = segment_ids[0]
    own_segment = lax.dynamic_slice_in_dim(segment, mp_index * own_rows, own_rows)
    first = jnp.sum((segment[None, :] < own_segment[:, None]).astype(jnp.int32), axis=1)
    positions = mp_index * own_rows + jnp.arange(own_rows, dtype=jnp.int32) - first
    frequency = rope_base ** (-(jnp.arange(HEAD // 2, dtype=F32) * 2.0) / HEAD)
    angles = positions.astype(F32)[:, None] * frequency[None, :]
    cosine, sine = jnp.cos(angles), jnp.sin(angles)
    cosine = jnp.concatenate([cosine, cosine], axis=1)
    sine = jnp.concatenate([-sine, sine], axis=1)

    by_head = kv_cotangent[0].reshape(own_rows, 8, 2, HEAD)
    halves = [by_head[:, :, h].reshape(own_rows, -1).astype(F32) for h in range(2)]
    own_back = [rotate(h, cosine, -sine).astype(BF) for h in halves]
    width = kv_weight.shape[0]
    weight_own = kv_weight.reshape(width, 8, 2, HEAD).transpose(0, 2, 1, 3).reshape(width, -1)
    weight_met = take(weight_own, 0, 0, 1)
    gain_own = norm_gain[None, :]
    gain_met = take(gain_own, 0, 0, 1)

    images = lax.all_to_all(image_tokens[0], "mp", split_axis=1, concat_axis=0, tiled=True)
    slots = jnp.where(
        jnp.arange(16, dtype=jnp.int32)[:, None] == mp_index, image_slots[0][None, :], 0
    )
    slots = chip_sum(slots + take(slots, 0, 0, 1)).reshape(1, -1)

    back = [gather_rows(b) for b in own_back]

    own, other = build_hidden(place, slots, images, text_embeds[0])
    met = take(other, 0, 0, 1)
    terms = [
        project(own, met, gain_own, gain_met, weight_own, weight_met, part) for part in range(2)
    ]

    def to_chips(values):
        spread = jnp.where(
            chips[:, None, None] == jnp.arange(8)[None, :, None], values.reshape(8, 1, -1), 0.0
        )
        return jnp.sum(spread, axis=0)

    def from_chips(values):
        spread = jnp.where(chips[:, None, None] == jnp.arange(8)[None, :, None], values[None], 0.0)
        return jnp.sum(spread, axis=1)

    squares = jnp.sum(jnp.square(own.astype(F32)), axis=1) + jnp.sum(
        jnp.square(met.astype(F32)), axis=1
    )
    squares = from_chips(chip_sum(to_chips(squares)))
    inverse_rms = lax.rsqrt(squares / D + epsilon_value)
    scale = inverse_rms.reshape(-1, 1)

    projected = [reduce_rows(t) for t in terms]

    own_scale = inverse_rms[7][:, None]
    states = []
    bias = kv_bias.reshape(8, 2, HEAD)
    for h in range(2):
        shifted = projected[h] * own_scale + bias[:, h].reshape(1, -1)
        states.append(rotate(shifted, cosine, sine).astype(BF).reshape(own_rows, 8, HEAD))
    states = jnp.stack(states, axis=2).reshape(own_rows, -1)

    sums = []
    for h in range(2):
        mine, sent = weight_grad(place, own, met, gain_own, gain_met, scale, back[h])
        mine = add(mine, take(sent, 0, 0, 1)).astype(BF)
        sums.append(phase_reduce([mine[:, j * HEAD : (j + 1) * HEAD] for j in range(8)]))
    kept = jnp.where(dp == 0, sums[0], sums[1])
    given = jnp.where(dp == 0, sums[1], sums[0]).astype(BF)
    parameter = kept + take_dp(given).astype(F32)
    weight_total = parameter[:width]
    bias_total = parameter[width]

    inner = sum(jnp.sum(add(b) * add(t), axis=1) for b, t in zip(back, terms))
    inner = from_chips(chip_sum(to_chips(inner)))
    pull = (inverse_rms**3 * inner / D).reshape(-1, 1)
    grad_own, grad_sent, gain_kept, gain_sent = hidden_grad(
        back[0], back[1], own, met, gain_own, gain_met, weight_own, weight_met, scale, pull
    )
    grad_other = take(grad_sent, 0, 0, 1)
    text_grad, image_rows = split_grads(place, slots, grad_own, grad_other)
    image_grad = lax.all_to_all(image_rows, "mp", split_axis=0, concat_axis=1, tiled=True)
    gain_total = gain_kept + take(gain_sent, 0, 0, 1)
    for bit in (1, 2, 4):
        gain_total = gain_total + take_phase_xor(gain_total, bit)
    gain_total = (gain_total + take_dp(gain_total))[0]
    return (states[None], text_grad[None], image_grad[None], weight_total, bias_total, gain_total)


def solution(mesh):
    return jax.shard_map(
        per_device,
        mesh=mesh,
        in_specs=(
            P(("phase", "dp"), None, "mp"),
            P(("phase", "dp"), "mp", None),
            P(("phase", "dp"), "mp"),
            P(("phase", "dp"), None),
            P("mp"),
            P("mp", None),
            P(),
            P(("phase", "dp"), "mp", None),
        ),
        out_specs=(
            P(("phase", "dp"), "mp", None),
            P(("phase", "dp"), None, "mp"),
            P(("phase", "dp"), "mp", None),
            P("mp", ("phase", "dp")),
            P(("phase", "dp")),
            P("mp"),
        ),
        check_vma=False,
    )
```

```python
import jax
import jax.numpy as jnp
import numpy as np
from jax import lax
from jax.experimental import pallas as pl
from jax.experimental.pallas import tpu as pltpu
from jax.sharding import PartitionSpec as P

D = 8192
HEAD = 128
PAD = 56
epsilon_value = 1e-06
rope_base = 1000000.0

BF = jnp.bfloat16
F32 = jnp.float32
MIB = 1 << 20
HIGH = lax.Precision.HIGHEST

ORDER = ((0, 0), (0, 1), (0, 3), (0, 2), (1, 0), (1, 1), (1, 3), (1, 2))


def take(value, dy, dx, dc=0):
    pairs = []
    for y in range(2):
        for x in range(4):
            for c in range(2):
                source = (((y + dy) % 2) * 4 + (x + dx) % 4) * 2 + (c + dc) % 2
                pairs.append((source, (y * 4 + x) * 2 + c))
    return lax.ppermute(value, "mp", pairs)


def swap_core(value):
    return take(value, 0, 0, 1)


def exchange(value):
    return lax.all_to_all(value, "mp", split_axis=0, concat_axis=0, tiled=True)


def spread(row, out):
    for k in range(out.shape[0]):
        out[k] = row


def gather_sum(terms):
    total = terms[0]
    for k in range(1, terms.shape[0]):
        total = total + terms[k]
    return total


def gather_rows(block):
    right, left, far = take(block, 0, 1), take(block, 0, 3), take(block, 0, 2)
    across = take(block, 1, 0)
    return [
        block, right, left, far,
        across, take(across, 0, 1), take(across, 0, 3), take(far, 1, 0),
    ]


def add(*values):
    total = values[0].astype(F32)
    for value in values[1:]:
        total = total + value.astype(F32)
    return total.astype(BF)


def reduce_rows(terms):
    here, right, left, far, across, across_right, across_left, across_far = terms
    one, two = take(across_right, 0, 3), take(across_left, 0, 1)
    over = take(across_far, 1, 0)
    return (one, two, over), (here, take(right, 0, 3), take(left, 0, 1))


def local_call(kernel, micros, inputs, out_shape, after=(), far=(), scratch=(), lazy=False):
    near, distant, extra = len(inputs), len(far), len(after)
    outs = len(out_shape)
    results = [k for k, entry in enumerate(out_shape) if len(entry) > 2]

    def body(*refs):
        given, held = list(refs[:near]), refs[near : near + distant]
        refs = refs[near + distant + extra :]
        out, refs = list(refs[:outs]), refs[outs:]
        stages, refs = refs[:distant], refs[distant:]
        homes, refs = refs[: len(results)], refs[len(results) :]
        copies = [
            pltpu.make_async_copy(source, stage, refs[-1].at[k])
            for k, (source, stage) in enumerate(zip(held, stages))
        ]
        for copy in copies:
            copy.start()
        if not lazy:
            for copy in copies:
                copy.wait()
        targets = [out[k] for k in results]
        for k, home in zip(results, homes):
            out[k] = home
        back = [
            pltpu.make_async_copy(home, target, refs[-1].at[distant + k])
            for k, (home, target) in enumerate(zip(homes, targets))
        ]
        used = refs[:-1] if distant or results else refs
        if lazy:
            kernel(copies, back, *given, *stages, *out, *used)
        else:
            kernel(*given, *stages, *out, *used)
            for copy in back:
                copy.start()
        for copy in back:
            copy.wait()

    vmem = pl.BlockSpec(memory_space=pltpu.VMEM)
    smem = pl.BlockSpec(memory_space=pltpu.SMEM)
    hbm = pl.BlockSpec(memory_space=pltpu.HBM)
    staging = [pltpu.VMEM(value.shape, value.dtype) for value in far]
    staging += [pltpu.VMEM(*out_shape[k][:2]) for k in results]
    staging += [pltpu.VMEM(*entry) for entry in scratch]
    if distant or results:
        staging.append(pltpu.SemaphoreType.DMA((distant + len(results),)))
    return pl.pallas_call(
        body,
        in_specs=[smem if value.ndim == 1 else vmem for value in inputs] + [hbm] * (distant + extra),
        out_specs=[hbm if len(entry) > 2 else vmem for entry in out_shape],
        out_shape=[jax.ShapeDtypeStruct(*entry[:2]) for entry in out_shape],
        scratch_shapes=staging,
        compiler_params=pltpu.CompilerParams(vmem_limit_bytes=60 * MIB),
        cost_estimate=pl.CostEstimate(
            flops=int(micros * 1.15e9), bytes_accessed=int(micros * 3.6e6), transcendentals=0
        ),
        name=kernel.__name__.removesuffix("_kernel"),
    )(*inputs, *far, *after)


def turn(values, cosine, sine):
    half = HEAD // 2
    swapped = jnp.concatenate([values[:, half:], values[:, :half]], axis=1)
    return values * cosine + swapped * sine


def back_kernel(index, segment, frequency, cotangent, out, cosine_out, sine_out):
    rows, length = cotangent.shape[0], segment.shape[1]
    base = index[0] * rows
    ids = segment[...]
    row = base + lax.broadcasted_iota(jnp.int32, (rows, length), 0)
    here = row == lax.broadcasted_iota(jnp.int32, (rows, length), 1)
    ids_wide = jnp.broadcast_to(ids, (rows, length)).astype(F32)
    own = jnp.sum(jnp.where(here, ids_wide, 0.0), axis=1, keepdims=True)
    first = jnp.sum(jnp.where(ids_wide < own, 1.0, 0.0), axis=1, keepdims=True)
    position = (row[:, :1]).astype(F32) - first
    angle = position * frequency[...]
    cosine = jnp.cos(angle)
    sign = jnp.where(
        lax.broadcasted_iota(jnp.int32, (rows, HEAD), 1) < HEAD // 2, -1.0, 1.0
    )
    sine = jnp.sin(angle) * sign
    cosine_out[...] = cosine
    sine_out[...] = sine
    heads = cotangent.shape[1] // HEAD
    for head in range(heads):
        value = cotangent[:, head * HEAD : (head + 1) * HEAD]
        if head < heads // 2:
            value = turn(value.astype(F32), cosine, -sine).astype(BF)
        out[:, head * HEAD : (head + 1) * HEAD] = value


def make_back(index, segment, frequency, cotangent):
    rows, columns = cotangent.shape
    return local_call(
        back_kernel,
        2,
        (index, segment, frequency, cotangent),
        [((rows, columns), BF, 1)] + [((rows, HEAD), F32, 1)] * 2,
    )


def tiles_kernel(digits, image, out):
    width = out.shape[2]
    extra = out.shape[1] - image.shape[0]
    first = lax.broadcasted_iota(jnp.int32, (extra, width), 0) == 0
    tail = jnp.where(first, digits[...], 0.0)
    for j in range(out.shape[0]):
        block = image[:, j * width : (j + 1) * width].astype(F32)
        out[j] = jnp.concatenate([block, tail], axis=0).astype(BF)


def make_tiles(image, digits, after):
    width = digits.shape[1]
    return local_call(
        tiles_kernel, 2, (digits,), [((image.shape[1] // width, PAD, width), BF, 1)], after, (image,)
    )[0]


def hidden_kernel(place, slots, images, text, own, other, squares):
    count = slots.shape[1]
    rows = text.shape[0] // 8
    half = rows // 2
    core = place[8]
    line = lax.broadcasted_iota(jnp.int32, (rows, count), 0)
    for j in range(8):
        start = pl.multiple_of(place[j] * rows, rows)
        hit = (start + line == slots[...]).astype(F32)
        picked = jnp.dot(hit.astype(BF), images[...], preferred_element_type=F32)
        named = jnp.max(hit, axis=1, keepdims=True) > 0.5
        hidden = jnp.where(named, picked, text[pl.ds(start, rows), :].astype(F32))
        top, low = hidden[:half], hidden[half:]
        block = slice(j * half, (j + 1) * half)
        own[block] = jnp.where(core == 0, top, low).astype(BF)
        other[block] = jnp.where(core == 0, low, top).astype(BF)
        sums = jnp.concatenate([as_row(lanes(top * top)), as_row(lanes(low * low))], axis=1)
        for k in range(squares.shape[0]):
            squares[k, :, pl.ds(start, rows)] = sums


def build_hidden(place, slots, images, text, after):
    rows, width = text.shape
    return local_call(
        hidden_kernel,
        5,
        (place, slots),
        [((rows // 2, width), BF, 1)] * 2 + [((16, 1, rows), F32, 1)],
        after,
        (images, text),
    )


def lanes(values):
    total = values[:, :HEAD]
    for k in range(1, values.shape[1] // HEAD):
        total = total + values[:, k * HEAD : (k + 1) * HEAD]
    return total


def as_row(partial):
    return jnp.sum(partial.T, axis=0, keepdims=True)


def as_column(row):
    return jnp.broadcast_to(row, (HEAD, HEAD)).T


def part_of(place, j, rows):
    return pl.ds(pl.multiple_of(place[j] * rows, rows), rows)


def project_kernel(
    ready, done, gain_own, gain_met, own, met, weight_own, weight_met, *refs
):
    *out, scaled_own, scaled_met = refs
    rows = out[0].shape[0]
    columns = weight_own.shape[1]
    for copy in ready[:2]:
        copy.wait()
    scaled_own[...] = (own[...].astype(F32) * gain_own[...]).astype(BF)
    scaled_met[...] = (met[...].astype(F32) * gain_met[...]).astype(BF)
    for copy in ready[2:]:
        copy.wait()
    for j in range(0, 8, 4):
        block = slice(j * rows, (j + 4) * rows)
        for n in range(0, columns, 512):
            part = slice(n, n + 512)
            total = (
                jnp.dot(scaled_own[block], weight_own[:, part], preferred_element_type=F32)
                + jnp.dot(scaled_met[block], weight_met[:, part], preferred_element_type=F32)
            ).astype(BF)
            for k in range(4):
                out[j + k][:, part] = total[k * rows : (k + 1) * rows]
        for k in range(4):
            done[j + k].start()


def project(own, met, gain_own, gain_met, weight_own, weight_met):
    rows, width = own.shape
    columns = weight_own.shape[1]
    return local_call(
        project_kernel,
        16,
        (gain_own, gain_met),
        [((rows // 8, columns), BF, 1)] * 8,
        far=(own, met, weight_own, weight_met),
        scratch=[((rows, width), BF)] * 2,
        lazy=True,
    )


def normalize_kernel(
    place, gain_own, gain_met, squares, own, met, out_own, out_met, scale_out, sums
):
    rows = own.shape[0] // 8
    sums[...] = gather_sum(squares)
    core = place[8]
    for j in range(8):
        block = slice(j * rows, (j + 1) * rows)
        start = pl.multiple_of((2 * place[j] + core) * rows, rows)
        total = sums[:, pl.ds(start, rows)]
        scale = as_column(lax.rsqrt(total / D + epsilon_value))
        scale_out[block] = scale
        wide = jnp.concatenate([scale] * (own.shape[1] // HEAD), axis=1)
        for source, gain, out in ((own, gain_own, out_own), (met, gain_met, out_met)):
            out[:, block] = (source[block].astype(F32) * wide * gain[...]).astype(BF).T


def normalize(place, gain_own, gain_met, squares, own, met, after):
    rows, width = own.shape
    return local_call(
        normalize_kernel,
        3,
        (place, gain_own, gain_met, squares),
        [((width, rows), BF, 1)] * 2 + [((rows, HEAD), F32, 1)],
        after,
        (own, met),
        [((1, 2 * rows), F32)],
    )


def fill_weight_grad(normed, whole, bias, out):
    width, columns = normed.shape[0], whole.shape[1]
    first = lax.broadcasted_iota(jnp.int32, (16, columns), 0) == 0
    extra = jnp.where(first, bias, 0.0).astype(BF)
    share = columns // 8
    for j in range(0, 8, 2):
        total = jnp.dot(
            normed[...], whole[:, j * share : (j + 2) * share], preferred_element_type=F32
        ).astype(BF)
        for k in range(2):
            out[j + k, :width, :] = total[:, k * share : (k + 1) * share]
            out[j + k, width:, :] = extra[:, (j + k) * share : (j + k + 1) * share]


def weight_grad_own_kernel(ready, done, place, normed, *refs):
    back, terms, (out, inner, whole) = refs[:8], refs[8:16], refs[16:]
    rows, columns = back[0].shape
    bias = jnp.zeros((1, columns), F32)
    for j in range(8):
        ready[j + 1].wait()
        ready[j + 9].wait()
        whole[j * rows : (j + 1) * rows] = back[j][...]
        value = back[j][...].astype(F32)
        bias += jnp.sum(value, axis=0, keepdims=True)
        sums = as_row(lanes(value * terms[j][...].astype(F32)))
        start = pl.multiple_of(place[j] * rows, rows)
        for k in range(inner.shape[0]):
            inner[k, :, pl.ds(start, rows)] = sums
    done[1].start()
    ready[0].wait()
    fill_weight_grad(normed, whole, bias, out)
    done[0].start()


def weight_grad_own(place, normed, back, terms, after):
    width, rows = normed.shape
    columns = back[0].shape[1]
    return local_call(
        weight_grad_own_kernel,
        6,
        (place,),
        [((8, width + 16, columns // 8), BF, 1), ((16, 1, rows), F32, 1)],
        after,
        (normed, *back, *terms),
        [((rows, columns), BF)],
        lazy=True,
    )


def weight_grad_met_kernel(ready, done, normed, *refs):
    back, (far_term, across_term, one, two, over) = refs[:8], refs[8:13]
    out, far, across, whole = refs[13:]
    rows, columns = back[0].shape
    for copy in ready[9:]:
        copy.wait()
    far[...] = add(far_term[...], over[...])
    done[1].start()
    across[...] = add(across_term[...], one[...], two[...])
    done[2].start()
    bias = jnp.zeros((1, columns), F32)
    for j in range(8):
        ready[j + 1].wait()
        value = back[j][...]
        whole[j * rows : (j + 1) * rows] = value
        bias += jnp.sum(value.astype(F32), axis=0, keepdims=True)
    ready[0].wait()
    fill_weight_grad(normed, whole, bias, out)
    done[0].start()


def weight_grad_met(normed, back, terms, arrived, after):
    width, rows = normed.shape
    columns = back[0].shape[1]
    return local_call(
        weight_grad_met_kernel,
        5,
        (),
        [((8, width + 16, columns // 8), BF, 1)] + [((rows // 8, columns), BF, 1)] * 2,
        after,
        (normed, *back, *terms, *arrived),
        [((rows, columns), BF)],
        lazy=True,
    )


def hidden_grad_kernel(
    ready, done, gain_own, gain_met, own, met, weight_own, weight_met, scale, *refs
):
    back = refs[:8]
    grad_own, grad_met, sum_own, sum_met, whole = refs[8:]
    rows = back[0].shape[0]
    last = (((1,), (1,)), ((), ()))
    sum_own[...] = jnp.zeros_like(sum_own)
    sum_met[...] = jnp.zeros_like(sum_met)
    for j in range(0, 8, 4):
        block = slice(j * rows, (j + 4) * rows)
        for copy in ready[5 + j : 9 + j] + (ready[:5] if j == 0 else []):
            copy.wait()
        for k in range(j, j + 4):
            whole[k * rows : (k + 1) * rows] = back[k][...]
        s = jnp.concatenate([scale[block]] * 2, axis=1)
        for source, gain, weight, grad, total in (
            (met, gain_met, weight_met, grad_met, sum_met),
            (own, gain_own, weight_own, grad_own, sum_own),
        ):
            for n in range(0, own.shape[1], 256):
                part = slice(n, n + 256)
                scaled = s * lax.dot_general(
                    whole[block], weight[part], last, preferred_element_type=F32
                )
                grad[block, part] = (scaled * gain[:, part]).astype(BF)
                total[:, part] += jnp.sum(
                    scaled * source[block, part].astype(F32), axis=0, keepdims=True
                )
    for copy in done:
        copy.start()


def hidden_grad(own, met, gain_own, gain_met, weight_own, weight_met, scale, back, after):
    rows, width = own.shape
    columns = back[0].shape[1]
    return local_call(
        hidden_grad_kernel,
        9,
        (gain_own, gain_met),
        [((rows, width), BF, 1)] * 2 + [((1, width), F32)] * 2,
        after,
        (own, met, weight_own, weight_met, scale, *back),
        [((rows, columns), BF)],
        lazy=True,
    )


def split_kernel(
    place, slots, slot_lines, squares, inner,
    grad_own, grad_other, own, other, text, images, whole, pulls,
):
    count = slots.shape[1]
    core = place[8]
    half = own.shape[0] // 8
    rows = 2 * half
    width = own.shape[1]
    line = lax.broadcasted_iota(jnp.int32, (rows, count), 0)
    even, odd = inner[0], inner[1]
    for k in range(2, inner.shape[0], 2):
        even, odd = even + inner[k], odd + inner[k + 1]
    whole_inner = jnp.concatenate(
        [v[:, k * half : (k + 1) * half] for k in range(8) for v in (even, odd)], axis=1
    )
    scale = lax.rsqrt(gather_sum(squares) / D + epsilon_value)
    pull_row = scale * scale * scale * whole_inner / D
    pulls[...] = jnp.broadcast_to(pull_row, pulls.shape)
    for j in range(8):
        block = slice(j * half, (j + 1) * half)
        start = pl.multiple_of(place[j] * rows, rows)
        values = []
        for grad, hidden in ((grad_own, own), (grad_other, other)):
            values.append((grad[block].astype(F32), hidden[block].astype(F32)))
        (one, one_hidden), (two, two_hidden) = values
        value = jnp.concatenate(
            [jnp.where(core == 0, one, two), jnp.where(core == 0, two, one)], axis=0
        )
        hidden = jnp.concatenate(
            [
                jnp.where(core == 0, one_hidden, two_hidden),
                jnp.where(core == 0, two_hidden, one_hidden),
            ],
            axis=0,
        )
        near = pulls[:1, pl.ds(start, rows)]
        pull = jnp.concatenate([as_column(near[:, :half]), as_column(near[:, half:])], axis=0)
        value = value - hidden * jnp.concatenate([pull] * (width // HEAD), axis=1)
        hit = (start + line == slots[...]).astype(F32)
        named = jnp.max(hit, axis=1, keepdims=True) > 0.5
        whole[pl.ds(start, rows), :] = value.astype(BF)
        text[pl.ds(start, rows), :] = jnp.where(named, 0.0, value).astype(BF)
    tokens = whole.shape[0]
    for k in range(0, images.shape[0], 256):
        lines = slot_lines[k : k + 256]
        pick = (lax.broadcasted_iota(jnp.int32, (256, tokens), 1) == lines).astype(F32)
        images[k : k + 256] = jnp.dot(
            pick.astype(BF), whole[...], preferred_element_type=F32
        ).astype(BF)


def split_grads(
    place, slots, slot_lines, squares, inner, grad_own, grad_other, own, other, after,
):
    rows, width = own.shape
    count = slot_lines.shape[0]
    return local_call(
        split_kernel,
        5,
        (place, slots, slot_lines, squares, inner),
        [((2 * rows, width), BF, 1), ((count, width), BF, 1)],
        after,
        (grad_own, grad_other, own, other),
        [((2 * rows, width), BF), ((8, 2 * rows), F32)],
    )


def states_kernel(bias, here, left, right, far, across, scale, cosine, sine, out):
    c, s, factor = cosine[...], sine[...], scale[...]
    heads = out.shape[1] // HEAD
    for head in range(heads):
        block = slice(head * HEAD, (head + 1) * HEAD)
        value = here[:, block].astype(F32)
        for term in (left, right, far, across):
            value += term[:, block].astype(F32)
        value = value * factor + bias[:, block]
        if head < heads // 2:
            value = turn(value, c, s)
        out[:, block] = value.astype(BF)


def make_states(terms, scale, bias, cosine, sine):
    return local_call(
        states_kernel, 3, (bias,), [(terms[0].shape, BF, 1)], (), (*terms, scale, cosine, sine)
    )[0]


def join_kernel(tiles, out):
    width = tiles.shape[2]
    for j in range(tiles.shape[0]):
        out[:, j * width : (j + 1) * width] = tiles[j]


def join_tiles(tiles, after):
    count, rows, width = tiles.shape
    return local_call(join_kernel, 2, (), [((rows, count * width), BF, 1)], after, (tiles,))[0]


def per_device(
    text_embeds, image_tokens, image_slots, segment_ids, norm_gain, kv_weight, kv_bias, kv_cotangent
):
    mp_index = lax.axis_index("mp")
    dp = lax.axis_index("dp")
    index = mp_index.astype(jnp.int32)[None]
    core, column, line = mp_index % 2, (mp_index // 2) % 4, mp_index // 8
    place = [((line + dy) % 2) * 4 + (column + dx) % 4 for dy, dx in ORDER]
    place = jnp.stack(place + [core]).astype(jnp.int32)
    width = kv_weight.shape[0]
    count = image_slots.shape[1]

    frequency = rope_base ** (-(np.arange(HEAD // 2, dtype=np.float32) * np.float32(2.0)) / HEAD)
    frequency = np.concatenate([frequency, frequency]).astype(np.float32)[None, :]
    own_back, cosine, sine = make_back(
        index, segment_ids, jnp.asarray(frequency), kv_cotangent[0]
    )
    own_slots = image_slots[0]
    digits = jnp.concatenate([own_slots // 64, own_slots % 64]).astype(F32)
    digits = jnp.pad(digits[None, :], ((0, 0), (0, width - 2 * count)))
    images = exchange(make_tiles(image_tokens[0], digits, (own_back,)))

    back = gather_rows(own_back)

    weight_own = kv_weight
    weight_met = swap_core(weight_own)
    gain_own = norm_gain[None, :]
    gain_met = swap_core(gain_own)

    digits = images[:, count, :].astype(jnp.int32)
    found = digits[:, :count] * 64 + digits[:, count : 2 * count]
    slots = jnp.pad(found, ((0, 0), (0, PAD - count)), constant_values=-1).reshape(1, -1)

    own, other, squares = build_hidden(
        place, slots, images.reshape(-1, width), text_embeds[0], (back[1], back[2], back[4])
    )
    squares = exchange(squares)
    met = swap_core(other)
    terms = project(own, met, gain_own, gain_met, weight_own, weight_met)
    arrived, met_terms = reduce_rows(terms)
    normed_own, normed_met, scale = normalize(
        place, gain_own, gain_met, squares, own, met, terms[:1]
    )

    mine, inner = weight_grad_own(place, normed_own, back, terms, ())
    sent, far, across = weight_grad_met(
        normed_met, back, terms[3:5], arrived, (mine, *met_terms[1:])
    )
    met_terms = (*met_terms, take(far, 0, 2), take(across, 1, 0))
    inner = exchange(inner)
    met_mine = swap_core(sent)
    grad_own, grad_sent, gain_kept, gain_sent = hidden_grad(
        own, met, gain_own, gain_met, weight_own, weight_met, scale, back,
        (),
    )
    gain = (gain_kept + swap_core(gain_sent)).reshape(width // HEAD, HEAD)
    gain = jnp.concatenate([gain, gain], axis=1)
    gain = jnp.pad(gain, ((width + 1, mine.shape[1] - width - 1 - gain.shape[0]), (0, 0)))
    mine = (mine.astype(F32) + met_mine.astype(F32) + gain[None]).astype(BF)
    sums = lax.psum_scatter(mine, "phase", scatter_dimension=0, tiled=True)[0]
    kept = jnp.where(dp == 0, sums[:, :HEAD], sums[:, HEAD:]).astype(F32)
    given = jnp.where(dp == 0, sums[:, HEAD:], sums[:, :HEAD])
    parameter = kept + lax.ppermute(given, "dp", [(0, 1), (1, 0)]).astype(F32)
    weight_total = parameter[:width]
    bias_total = parameter[width]
    gain_total = parameter[width + 1 : width + 1 + width // HEAD].reshape(-1)

    rows = kv_cotangent.shape[1]
    states = make_states(met_terms, scale[:rows], kv_bias[None, :], cosine, sine)
    grad_other = swap_core(grad_sent)
    text_grad, image_rows = split_grads(
        place, slots, found.reshape(-1, 1), squares, inner,
        grad_own, grad_other, own, other, (),
    )
    image_tiles = exchange(image_rows.reshape(16, count, width))
    image_grad = join_tiles(image_tiles, (states, parameter))
    return (states[None], text_grad[None], image_grad[None], weight_total, bias_total, gain_total)


def solution(mesh):
    return jax.shard_map(
        per_device,
        mesh=mesh,
        in_specs=(
            P(("phase", "dp"), None, "mp"),
            P(("phase", "dp"), "mp", None),
            P(("phase", "dp"), "mp"),
            P(("phase", "dp"), None),
            P("mp"),
            P("mp", None),
            P(),
            P(("phase", "dp"), "mp", None),
        ),
        out_specs=(
            P(("phase", "dp"), "mp", None),
            P(("phase", "dp"), None, "mp"),
            P(("phase", "dp"), "mp", None),
            P("mp", ("phase", "dp")),
            P(("phase", "dp")),
            P("mp"),
        ),
        check_vma=False,
    )
```

```python
import jax
import jax.numpy as jnp
import numpy as np
from jax import lax
from jax.experimental import pallas as pl
from jax.experimental.pallas import tpu as pltpu
from jax.sharding import PartitionSpec as P

D = 8192
HEAD = 128
PAD = 56
epsilon_value = 1e-06
rope_base = 1000000.0

BF = jnp.bfloat16
F32 = jnp.float32
MIB = 1 << 20
HIGH = lax.Precision.HIGHEST

ORDER = ((0, 0), (0, 1), (0, 3), (0, 2), (1, 0), (1, 1), (1, 3), (1, 2))


def take(value, dy, dx, dc=0):
    pairs = []
    for y in range(2):
        for x in range(4):
            for c in range(2):
                source = (((y + dy) % 2) * 4 + (x + dx) % 4) * 2 + (c + dc) % 2
                pairs.append((source, (y * 4 + x) * 2 + c))
    return lax.ppermute(value, "mp", pairs)


def swap_core(value):
    return take(value, 0, 0, 1)


def exchange(value):
    return lax.all_to_all(value, "mp", split_axis=0, concat_axis=0, tiled=True)


def spread(row, out):
    for k in range(out.shape[0]):
        out[k] = row


def gather_sum(terms):
    total = terms[0]
    for k in range(1, terms.shape[0]):
        total = total + terms[k]
    return total


def gather_rows(block):
    right, left, far = take(block, 0, 1), take(block, 0, 3), take(block, 0, 2)
    across = take(block, 1, 0)
    return [
        block, right, left, far,
        across, take(across, 0, 1), take(across, 0, 3), take(far, 1, 0),
    ]


def add(*values):
    total = values[0].astype(F32)
    for value in values[1:]:
        total = total + value.astype(F32)
    return total.astype(BF)


def reduce_rows(terms):
    here, right, left, far, across, across_right, across_left, across_far = terms
    one, two = take(across_right, 0, 3), take(across_left, 0, 1)
    over = take(across_far, 1, 0)
    return (one, two, over), (here, take(right, 0, 3), take(left, 0, 1))


def take_phase(value, dz):
    return lax.ppermute(value, "phase", [((p + dz) % 8, p) for p in range(8)])


def reduce_phases(phase, mine, met, waits):
    def block(dz, *arrived):
        at = lax.rem(phase + dz, 8)
        own = lax.dynamic_index_in_dim(mine, at, 0, False).astype(F32)
        other = lax.dynamic_index_in_dim(met, at, 0, False).astype(F32)
        total = own + other
        for value in arrived:
            total = total + value.astype(F32)
        return total

    half = mine.shape[1] // 32 * 16
    rows = mine.shape[1]
    far = block(4).astype(BF)
    up = jnp.pad(take_phase(far[:half], -1), ((0, rows - half), (0, 0)))
    down = jnp.pad(take_phase(far[half:], 1), ((half, 0), (0, 0)))
    for step in (3, 2, 1):
        up, down, _ = lax.optimization_barrier((up, down, waits[step]))
        up = take_phase(block(step, up).astype(BF), -1)
        down = take_phase(block(8 - step, down).astype(BF), 1)
    up, down, _ = lax.optimization_barrier((up, down, waits[0]))
    return block(0, up, down)


def local_call(kernel, micros, inputs, out_shape, after=(), far=(), scratch=(), lazy=False):
    near, distant, extra = len(inputs), len(far), len(after)
    outs = len(out_shape)
    results = [k for k, entry in enumerate(out_shape) if len(entry) > 2]

    def body(*refs):
        given, held = list(refs[:near]), refs[near : near + distant]
        refs = refs[near + distant + extra :]
        out, refs = list(refs[:outs]), refs[outs:]
        stages, refs = refs[:distant], refs[distant:]
        homes, refs = refs[: len(results)], refs[len(results) :]
        copies = [
            pltpu.make_async_copy(source, stage, refs[-1].at[k])
            for k, (source, stage) in enumerate(zip(held, stages))
        ]
        for copy in copies:
            copy.start()
        if not lazy:
            for copy in copies:
                copy.wait()
        targets = [out[k] for k in results]
        for k, home in zip(results, homes):
            out[k] = home
        back = [
            pltpu.make_async_copy(home, target, refs[-1].at[distant + k])
            for k, (home, target) in enumerate(zip(homes, targets))
        ]
        used = refs[:-1] if distant or results else refs
        if lazy:
            kernel(copies, back, *given, *stages, *out, *used)
        else:
            kernel(*given, *stages, *out, *used)
            for copy in back:
                copy.start()
        for copy in back:
            copy.wait()

    vmem = pl.BlockSpec(memory_space=pltpu.VMEM)
    smem = pl.BlockSpec(memory_space=pltpu.SMEM)
    hbm = pl.BlockSpec(memory_space=pltpu.HBM)
    staging = [pltpu.VMEM(value.shape, value.dtype) for value in far]
    staging += [pltpu.VMEM(*out_shape[k][:2]) for k in results]
    staging += [pltpu.VMEM(*entry) for entry in scratch]
    if distant or results:
        staging.append(pltpu.SemaphoreType.DMA((distant + len(results),)))
    return pl.pallas_call(
        body,
        in_specs=[smem if value.ndim == 1 else vmem for value in inputs] + [hbm] * (distant + extra),
        out_specs=[hbm if len(entry) > 2 else vmem for entry in out_shape],
        out_shape=[jax.ShapeDtypeStruct(*entry[:2]) for entry in out_shape],
        scratch_shapes=staging,
        compiler_params=pltpu.CompilerParams(vmem_limit_bytes=60 * MIB),
        cost_estimate=pl.CostEstimate(
            flops=int(micros * 1.15e9), bytes_accessed=int(micros * 3.6e6), transcendentals=0
        ),
        name=kernel.__name__.removesuffix("_kernel"),
    )(*inputs, *far, *after)


def turn(values, cosine, sine):
    half = HEAD // 2
    swapped = jnp.concatenate([values[:, half:], values[:, :half]], axis=1)
    return values * cosine + swapped * sine


def back_kernel(index, segment, frequency, cotangent, out, cosine_out, sine_out):
    rows, length = cotangent.shape[0], segment.shape[1]
    base = index[0] * rows
    ids = segment[...]
    row = base + lax.broadcasted_iota(jnp.int32, (rows, length), 0)
    here = row == lax.broadcasted_iota(jnp.int32, (rows, length), 1)
    ids_wide = jnp.broadcast_to(ids, (rows, length)).astype(F32)
    own = jnp.sum(jnp.where(here, ids_wide, 0.0), axis=1, keepdims=True)
    first = jnp.sum(jnp.where(ids_wide < own, 1.0, 0.0), axis=1, keepdims=True)
    position = (row[:, :1]).astype(F32) - first
    angle = position * frequency[...]
    cosine = jnp.cos(angle)
    sign = jnp.where(
        lax.broadcasted_iota(jnp.int32, (rows, HEAD), 1) < HEAD // 2, -1.0, 1.0
    )
    sine = jnp.sin(angle) * sign
    cosine_out[...] = cosine
    sine_out[...] = sine
    heads = cotangent.shape[1] // HEAD
    for head in range(heads):
        value = cotangent[:, head * HEAD : (head + 1) * HEAD]
        if head < heads // 2:
            value = turn(value.astype(F32), cosine, -sine).astype(BF)
        out[:, head * HEAD : (head + 1) * HEAD] = value


def make_back(index, segment, frequency, cotangent):
    rows, columns = cotangent.shape
    return local_call(
        back_kernel,
        2,
        (index, segment, frequency, cotangent),
        [((rows, columns), BF, 1)] + [((rows, HEAD), F32, 1)] * 2,
    )


def tiles_kernel(slots, image, out, digits):
    width = out.shape[2]
    count = slots.shape[1]
    extra = out.shape[1] - image.shape[0]
    high = slots[...] >> 6
    digits[...] = jnp.zeros_like(digits)
    digits[:, :count] = high.astype(F32)
    digits[:, HEAD : HEAD + count] = (slots[...] - high * 64).astype(F32)
    first = lax.broadcasted_iota(jnp.int32, (extra, width), 0) == 0
    tail = jnp.where(first, digits[...], 0.0)
    for j in range(out.shape[0]):
        block = image[:, j * width : (j + 1) * width].astype(F32)
        out[j] = jnp.concatenate([block, tail], axis=0).astype(BF)


def make_tiles(image, slots, width):
    return local_call(
        tiles_kernel,
        2,
        (slots,),
        [((image.shape[1] // width, PAD, width), BF, 1)],
        (),
        (image,),
        [((1, width), F32)],
    )[0]


def hidden_kernel(place, slots, images, text, own, other, squares):
    count = slots.shape[1]
    rows = text.shape[0] // 8
    half = rows // 2
    core = place[8]
    line = lax.broadcasted_iota(jnp.int32, (rows, count), 0)
    for j in range(8):
        start = pl.multiple_of(place[j] * rows, rows)
        hit = (start + line == slots[...]).astype(F32)
        picked = jnp.dot(hit.astype(BF), images[...], preferred_element_type=F32)
        named = jnp.max(hit, axis=1, keepdims=True) > 0.5
        hidden = jnp.where(named, picked, text[pl.ds(start, rows), :].astype(F32))
        top, low = hidden[:half], hidden[half:]
        block = slice(j * half, (j + 1) * half)
        own[block] = jnp.where(core == 0, top, low).astype(BF)
        other[block] = jnp.where(core == 0, low, top).astype(BF)
        sums = jnp.concatenate([as_row(lanes(top * top)), as_row(lanes(low * low))], axis=1)
        for k in range(squares.shape[0]):
            squares[k, :, pl.ds(start, rows)] = sums


def build_hidden(place, slots, images, text, after):
    rows, width = text.shape
    return local_call(
        hidden_kernel,
        5,
        (place, slots),
        [((rows // 2, width), BF, 1)] * 2 + [((16, 1, rows), F32, 1)],
        after,
        (images, text),
    )


def lanes(values):
    total = values[:, :HEAD]
    for k in range(1, values.shape[1] // HEAD):
        total = total + values[:, k * HEAD : (k + 1) * HEAD]
    return total


def as_row(partial):
    return jnp.sum(partial.T, axis=0, keepdims=True)


def as_column(row):
    return jnp.broadcast_to(row, (HEAD, HEAD)).T


def part_of(place, j, rows):
    return pl.ds(pl.multiple_of(place[j] * rows, rows), rows)


def project_kernel(
    ready, done, gain_own, gain_met, own, met, weight_own, weight_met, *refs
):
    *out, scaled_own, scaled_met = refs
    rows = out[0].shape[0]
    columns = weight_own.shape[1]
    for copy in ready[:2]:
        copy.wait()
    scaled_own[...] = (own[...].astype(F32) * gain_own[...]).astype(BF)
    scaled_met[...] = (met[...].astype(F32) * gain_met[...]).astype(BF)
    for copy in ready[2:]:
        copy.wait()
    for j in range(0, 8, 4):
        block = slice(j * rows, (j + 4) * rows)
        for n in range(0, columns, 512):
            part = slice(n, n + 512)
            total = (
                jnp.dot(scaled_own[block], weight_own[:, part], preferred_element_type=F32)
                + jnp.dot(scaled_met[block], weight_met[:, part], preferred_element_type=F32)
            ).astype(BF)
            for k in range(4):
                out[j + k][:, part] = total[k * rows : (k + 1) * rows]
        for k in range(4):
            done[j + k].start()


def project(own, met, gain_own, gain_met, weight_own, weight_met):
    rows, width = own.shape
    columns = weight_own.shape[1]
    return local_call(
        project_kernel,
        60,
        (gain_own, gain_met),
        [((rows // 8, columns), BF, 1)] * 8,
        far=(own, met, weight_own, weight_met),
        scratch=[((rows, width), BF)] * 2,
        lazy=True,
    )


def normed_lines(source, scale, gain, out):
    rows = source.shape[0] // 8
    for j in range(8):
        block = slice(j * rows, (j + 1) * rows)
        wide = jnp.concatenate([scale[block]] * (source.shape[1] // HEAD), axis=1)
        out[:, block] = (source[block].astype(F32) * wide * gain[...]).astype(BF).T


def fill_weight_grad(normed, whole, out):
    width, columns = normed.shape[0], whole.shape[1]
    share = columns // 8
    for j in range(0, 8, 2):
        total = jnp.dot(
            normed[...], whole[:, j * share : (j + 2) * share], preferred_element_type=F32
        ).astype(BF)
        for k in range(2):
            out[j + k, :width, :] = total[:, k * share : (k + 1) * share]


def fill_extra(bias, gain, out):
    width, share = gain.shape[1], out.shape[2]
    line = lax.broadcasted_iota(jnp.int32, (16, share), 0)
    lines = jnp.zeros((16, share), F32)
    for k in range(width // HEAD):
        part = gain[:, k * HEAD : (k + 1) * HEAD]
        lines = jnp.where(line == k + 1, jnp.concatenate([part, part], axis=1), lines)
    for j in range(8):
        extra = jnp.where(line == 0, bias[:, j * share : (j + 1) * share], lines)
        out[j, width:, :] = extra.astype(BF)


def own_grads_kernel(ready, done, place, gain_own, gain_met, squares, own, *refs):
    back, terms, (met, weight_own, weight_met) = refs[:16:2], refs[1:16:2], refs[16:19]
    out, inner, scale, grad_own, grad_met, sum_met, whole, normed, sums, sum_own = refs[19:]
    rows, columns = back[0].shape
    core = place[8]
    sums[...] = gather_sum(squares)
    for j in range(8):
        start = pl.multiple_of((2 * place[j] + core) * rows, rows)
        total = sums[:, pl.ds(start, rows)]
        scale[j * rows : (j + 1) * rows] = as_column(lax.rsqrt(total / D + epsilon_value))
    done[2].start()
    ready[0].wait()
    normed_lines(own, scale, gain_own, normed)
    bias = jnp.zeros((1, columns), F32)
    for j in range(8):
        ready[2 * j + 1].wait()
        ready[2 * j + 2].wait()
        whole[j * rows : (j + 1) * rows] = back[j][...]
        value = back[j][...].astype(F32)
        bias += jnp.sum(value, axis=0, keepdims=True)
        line = as_row(lanes(value * terms[j][...].astype(F32)))
        start = pl.multiple_of(place[j] * rows, rows)
        for k in range(inner.shape[0]):
            inner[k, :, pl.ds(start, rows)] = line
    done[1].start()
    fill_weight_grad(normed, whole, out)
    for copy in ready[17:]:
        copy.wait()
    last = (((1,), (1,)), ((), ()))
    sum_own[...] = jnp.zeros_like(sum_own)
    sum_met[...] = jnp.zeros_like(sum_met)
    for source, gain, weight, grad, total, copy in (
        (met, gain_met, weight_met, grad_met, sum_met, done[4]),
        (own, gain_own, weight_own, grad_own, sum_own, done[3]),
    ):
        for j in range(0, 8, 4):
            block = slice(j * rows, (j + 4) * rows)
            s = jnp.concatenate([scale[block]] * 2, axis=1)
            for n in range(0, own.shape[1], 256):
                part = slice(n, n + 256)
                scaled = s * lax.dot_general(
                    whole[block], weight[part], last, preferred_element_type=F32
                )
                grad[block, part] = (scaled * gain[:, part]).astype(BF)
                total[:, part] += jnp.sum(
                    scaled * source[block, part].astype(F32), axis=0, keepdims=True
                )
        copy.start()
    fill_extra(bias, sum_own[...], out)
    done[0].start()


def own_grads(
    place, gain_own, gain_met, squares, own, met, weight_own, weight_met, back, terms
):
    rows, width = own.shape
    columns = back[0].shape[1]
    pieces = [value for pair in zip(back, terms) for value in pair]
    return local_call(
        own_grads_kernel,
        14,
        (place, gain_own, gain_met, squares),
        [
            ((8, width + 16, columns // 8), BF, 1),
            ((16, 1, rows), F32, 1),
            ((rows, HEAD), F32, 1),
            ((rows, width), BF, 1),
            ((rows, width), BF, 1),
            ((1, width), F32),
        ],
        (),
        (own, *pieces, met, weight_own, weight_met),
        [((rows, columns), BF), ((width, rows), BF), ((1, 2 * rows), F32), ((1, width), F32)],
        lazy=True,
    )


def met_grads_kernel(ready, done, gain, gain_sum, met, scale, *refs):
    back, (far_term, across_term, one, two, over) = refs[:8], refs[8:13]
    out, far, across, whole, normed = refs[13:]
    rows, columns = back[0].shape
    for copy in ready[:2]:
        copy.wait()
    normed_lines(met, scale, gain, normed)
    bias = jnp.zeros((1, columns), F32)
    for j in range(8):
        ready[j + 2].wait()
        value = back[j][...]
        whole[j * rows : (j + 1) * rows] = value
        bias += jnp.sum(value.astype(F32), axis=0, keepdims=True)
    fill_weight_grad(normed, whole, out)
    fill_extra(bias, gain_sum[...], out)
    done[0].start()
    for copy in ready[10:]:
        copy.wait()
    far[...] = add(far_term[...], over[...])
    done[1].start()
    across[...] = add(across_term[...], one[...], two[...])
    done[2].start()


def met_grads(gain, gain_sum, met, scale, back, terms, arrived):
    rows, width = met.shape
    columns = back[0].shape[1]
    return local_call(
        met_grads_kernel,
        6,
        (gain, gain_sum),
        [((8, width + 16, columns // 8), BF, 1)] + [((rows // 8, columns), BF, 1)] * 2,
        (),
        (met, scale, *back, *terms, *arrived),
        [((rows, columns), BF), ((width, rows), BF)],
        lazy=True,
    )


def split_kernel(
    place, slots, slot_lines, squares, inner,
    grad_own, grad_other, own, other, text, images, whole, pulls,
):
    count = slots.shape[1]
    core = place[8]
    half = own.shape[0] // 8
    rows = 2 * half
    width = own.shape[1]
    line = lax.broadcasted_iota(jnp.int32, (rows, count), 0)
    even, odd = inner[0], inner[1]
    for k in range(2, inner.shape[0], 2):
        even, odd = even + inner[k], odd + inner[k + 1]
    whole_inner = jnp.concatenate(
        [v[:, k * half : (k + 1) * half] for k in range(8) for v in (even, odd)], axis=1
    )
    scale = lax.rsqrt(gather_sum(squares) / D + epsilon_value)
    pull_row = scale * scale * scale * whole_inner / D
    pulls[...] = jnp.broadcast_to(pull_row, pulls.shape)
    for j in range(8):
        block = slice(j * half, (j + 1) * half)
        start = pl.multiple_of(place[j] * rows, rows)
        values = []
        for grad, hidden in ((grad_own, own), (grad_other, other)):
            values.append((grad[block].astype(F32), hidden[block].astype(F32)))
        (one, one_hidden), (two, two_hidden) = values
        value = jnp.concatenate(
            [jnp.where(core == 0, one, two), jnp.where(core == 0, two, one)], axis=0
        )
        hidden = jnp.concatenate(
            [
                jnp.where(core == 0, one_hidden, two_hidden),
                jnp.where(core == 0, two_hidden, one_hidden),
            ],
            axis=0,
        )
        near = pulls[:1, pl.ds(start, rows)]
        pull = jnp.concatenate([as_column(near[:, :half]), as_column(near[:, half:])], axis=0)
        value = value - hidden * jnp.concatenate([pull] * (width // HEAD), axis=1)
        hit = (start + line == slots[...]).astype(F32)
        named = jnp.max(hit, axis=1, keepdims=True) > 0.5
        whole[pl.ds(start, rows), :] = value.astype(BF)
        text[pl.ds(start, rows), :] = jnp.where(named, 0.0, value).astype(BF)
    tokens = whole.shape[0]
    for k in range(0, images.shape[0], 256):
        lines = slot_lines[k : k + 256]
        pick = (lax.broadcasted_iota(jnp.int32, (256, tokens), 1) == lines).astype(F32)
        images[k : k + 256] = jnp.dot(
            pick.astype(BF), whole[...], preferred_element_type=F32
        ).astype(BF)


def split_grads(
    place, slots, slot_lines, squares, inner, grad_own, grad_other, own, other, after,
):
    rows, width = own.shape
    count = slot_lines.shape[0]
    return local_call(
        split_kernel,
        5,
        (place, slots, slot_lines, squares, inner),
        [((2 * rows, width), BF, 1), ((count, width), BF, 1)],
        after,
        (grad_own, grad_other, own, other),
        [((2 * rows, width), BF), ((8, 2 * rows), F32)],
    )


def states_kernel(bias, here, left, right, far, across, scale, cosine, sine, out):
    c, s, factor = cosine[...], sine[...], scale[: out.shape[0]]
    heads = out.shape[1] // HEAD
    for head in range(heads):
        block = slice(head * HEAD, (head + 1) * HEAD)
        value = here[:, block].astype(F32)
        for term in (left, right, far, across):
            value += term[:, block].astype(F32)
        value = value * factor + bias[:, block]
        if head < heads // 2:
            value = turn(value, c, s)
        out[:, block] = value.astype(BF)


def make_states(terms, scale, bias, cosine, sine):
    return local_call(
        states_kernel, 3, (bias,), [(terms[0].shape, BF, 1)], (), (*terms, scale, cosine, sine)
    )[0]


def join_kernel(tiles, out):
    width = tiles.shape[2]
    for j in range(tiles.shape[0]):
        out[:, j * width : (j + 1) * width] = tiles[j]


def join_tiles(tiles, after):
    count, rows, width = tiles.shape
    return local_call(join_kernel, 2, (), [((rows, count * width), BF, 1)], after, (tiles,))[0]


def per_device(
    text_embeds, image_tokens, image_slots, segment_ids, norm_gain, kv_weight, kv_bias, kv_cotangent
):
    mp_index = lax.axis_index("mp")
    dp, phase = lax.axis_index("dp"), lax.axis_index("phase")
    index = mp_index.astype(jnp.int32)[None]
    core, column, line = mp_index % 2, (mp_index // 2) % 4, mp_index // 8
    place = [((line + dy) % 2) * 4 + (column + dx) % 4 for dy, dx in ORDER]
    place = jnp.stack(place + [core]).astype(jnp.int32)
    width = kv_weight.shape[0]
    count = image_slots.shape[1]

    frequency = rope_base ** (-(np.arange(HEAD // 2, dtype=np.float32) * np.float32(2.0)) / HEAD)
    frequency = np.concatenate([frequency, frequency]).astype(np.float32)[None, :]
    own_back, cosine, sine = make_back(
        index, segment_ids, jnp.asarray(frequency), kv_cotangent[0]
    )
    images = exchange(make_tiles(image_tokens[0], image_slots, width))

    back = gather_rows(own_back)

    weight_own = kv_weight
    weight_met = swap_core(weight_own)
    gain_own = norm_gain[None, :]
    gain_met = swap_core(gain_own)

    digits = images[:, count, :].astype(jnp.int32)
    found = digits[:, :count] * 64 + digits[:, HEAD : HEAD + count]
    slots = jnp.pad(found, ((0, 0), (0, PAD - count)), constant_values=-1).reshape(1, -1)

    own, other, squares = build_hidden(
        place, slots, images.reshape(-1, width), text_embeds[0], (back[1], back[2], back[4])
    )
    squares = exchange(squares)
    met = swap_core(other)
    terms = project(own, met, gain_own, gain_met, weight_own, weight_met)
    arrived, met_terms = reduce_rows(terms)
    mine, inner, scale, grad_own, grad_sent, gain_sum = own_grads(
        place, gain_own, gain_met, squares, own, met, weight_own, weight_met, back, terms
    )
    sent, far, across = met_grads(
        gain_met, gain_sum, met, scale, back, terms[3:5], arrived
    )
    met_terms = (*met_terms, take(far, 0, 2), take(across, 1, 0))
    inner = exchange(inner)
    met_mine = swap_core(sent)
    states = make_states(met_terms, scale, kv_bias[None, :], cosine, sine)
    grad_other = swap_core(grad_sent)
    text_grad, image_rows = split_grads(
        place, slots, found.reshape(-1, 1), squares, inner,
        grad_own, grad_other, own, other, (),
    )
    image_tiles = exchange(image_rows.reshape(16, count, width))
    waits = {3: inner, 2: (text_grad, *met_terms[1:3]), 1: met_terms[3:], 0: (image_tiles, states)}
    sums = reduce_phases(phase, mine, met_mine, waits)
    kept = jnp.where(dp == 0, sums[:, :HEAD], sums[:, HEAD:])
    given = jnp.where(dp == 0, sums[:, HEAD:], sums[:, :HEAD]).astype(BF)
    parameter = kept + lax.ppermute(given, "dp", [(0, 1), (1, 0)]).astype(F32)
    weight_total = parameter[:width]
    bias_total = parameter[width]
    gain_total = parameter[width + 1 : width + 1 + width // HEAD].reshape(-1)
    image_grad = join_tiles(image_tiles, ())
    return (states[None], text_grad[None], image_grad[None], weight_total, bias_total, gain_total)


def solution(mesh):
    return jax.shard_map(
        per_device,
        mesh=mesh,
        in_specs=(
            P(("phase", "dp"), None, "mp"),
            P(("phase", "dp"), "mp", None),
            P(("phase", "dp"), "mp"),
            P(("phase", "dp"), None),
            P("mp"),
            P("mp", None),
            P(),
            P(("phase", "dp"), "mp", None),
        ),
        out_specs=(
            P(("phase", "dp"), "mp", None),
            P(("phase", "dp"), None, "mp"),
            P(("phase", "dp"), "mp", None),
            P("mp", ("phase", "dp")),
            P(("phase", "dp")),
            P("mp"),
        ),
        check_vma=False,
    )
```

```python
import jax
import jax.numpy as jnp
import numpy as np
from jax import lax
from jax.experimental import pallas as pl
from jax.experimental.pallas import tpu as pltpu
from jax.sharding import PartitionSpec as P

D = 8192
HEAD = 128
PAD = 56
epsilon_value = 1e-06
rope_base = 1000000.0

BF = jnp.bfloat16
F32 = jnp.float32
MIB = 1 << 20
HIGH = lax.Precision.HIGHEST

ORDER = ((0, 0), (0, 1), (0, 3), (0, 2), (1, 0), (1, 1), (1, 3), (1, 2))


def take(value, dy, dx, dc=0):
    pairs = []
    for y in range(2):
        for x in range(4):
            for c in range(2):
                source = (((y + dy) % 2) * 4 + (x + dx) % 4) * 2 + (c + dc) % 2
                pairs.append((source, (y * 4 + x) * 2 + c))
    return lax.ppermute(value, "mp", pairs)


def swap_core(value):
    return take(value, 0, 0, 1)


def exchange(value):
    return lax.all_to_all(value, "mp", split_axis=0, concat_axis=0, tiled=True)


def spread(row, out):
    for k in range(out.shape[0]):
        out[k] = row


def gather_sum(terms):
    total = terms[0]
    for k in range(1, terms.shape[0]):
        total = total + terms[k]
    return total


def gather_rows(block):
    right, left, far = take(block, 0, 1), take(block, 0, 3), take(block, 0, 2)
    across = take(block, 1, 0)
    return [
        block, right, left, far,
        across, take(across, 0, 1), take(across, 0, 3), take(far, 1, 0),
    ]


def add(*values):
    total = values[0].astype(F32)
    for value in values[1:]:
        total = total + value.astype(F32)
    return total.astype(BF)


def reduce_rows(terms):
    here, right, left, far, across, across_right, across_left, across_far = terms
    one, two = take(across_right, 0, 3), take(across_left, 0, 1)
    over = take(across_far, 1, 0)
    return (one, two, over), (here, take(right, 0, 3), take(left, 0, 1))


def take_phase(value, dz):
    return lax.ppermute(value, "phase", [((p + dz) % 8, p) for p in range(8)])


def reduce_phases(phase, mine, met, waits):
    def block(dz, *arrived):
        at = lax.rem(phase + dz, 8)
        own = lax.dynamic_index_in_dim(mine, at, 0, False).astype(F32)
        other = lax.dynamic_index_in_dim(met, at, 0, False).astype(F32)
        total = own + other
        for value in arrived:
            total = total + value.astype(F32)
        return total

    half = mine.shape[1] // 32 * 16
    rows = mine.shape[1]
    far = block(4).astype(BF)
    up = jnp.pad(take_phase(far[:half], -1), ((0, rows - half), (0, 0)))
    down = jnp.pad(take_phase(far[half:], 1), ((half, 0), (0, 0)))
    for step in (3, 2, 1):
        up, down, _ = lax.optimization_barrier((up, down, waits[step]))
        up = take_phase(block(step, up).astype(BF), -1)
        down = take_phase(block(8 - step, down).astype(BF), 1)
    up, down, _ = lax.optimization_barrier((up, down, waits[0]))
    return block(0, up, down)


def local_call(kernel, micros, inputs, out_shape, after=(), far=(), scratch=(), lazy=False):
    near, distant, extra = len(inputs), len(far), len(after)
    outs = len(out_shape)
    results = [k for k, entry in enumerate(out_shape) if len(entry) > 2]

    def body(*refs):
        given, held = list(refs[:near]), refs[near : near + distant]
        refs = refs[near + distant + extra :]
        out, refs = list(refs[:outs]), refs[outs:]
        stages, refs = refs[:distant], refs[distant:]
        homes, refs = refs[: len(results)], refs[len(results) :]
        copies = [
            pltpu.make_async_copy(source, stage, refs[-1].at[k])
            for k, (source, stage) in enumerate(zip(held, stages))
        ]
        for copy in copies:
            copy.start()
        if not lazy:
            for copy in copies:
                copy.wait()
        targets = [out[k] for k in results]
        for k, home in zip(results, homes):
            out[k] = home
        back = [
            pltpu.make_async_copy(home, target, refs[-1].at[distant + k])
            for k, (home, target) in enumerate(zip(homes, targets))
        ]
        used = refs[:-1] if distant or results else refs
        if lazy:
            kernel(copies, back, *given, *stages, *out, *used)
        else:
            kernel(*given, *stages, *out, *used)
            for copy in back:
                copy.start()
        for copy in back:
            copy.wait()

    vmem = pl.BlockSpec(memory_space=pltpu.VMEM)
    smem = pl.BlockSpec(memory_space=pltpu.SMEM)
    hbm = pl.BlockSpec(memory_space=pltpu.HBM)
    staging = [pltpu.VMEM(value.shape, value.dtype) for value in far]
    staging += [pltpu.VMEM(*out_shape[k][:2]) for k in results]
    staging += [pltpu.VMEM(*entry) for entry in scratch]
    if distant or results:
        staging.append(pltpu.SemaphoreType.DMA((distant + len(results),)))
    return pl.pallas_call(
        body,
        in_specs=[smem if value.ndim == 1 else vmem for value in inputs] + [hbm] * (distant + extra),
        out_specs=[hbm if len(entry) > 2 else vmem for entry in out_shape],
        out_shape=[jax.ShapeDtypeStruct(*entry[:2]) for entry in out_shape],
        scratch_shapes=staging,
        compiler_params=pltpu.CompilerParams(vmem_limit_bytes=60 * MIB),
        cost_estimate=pl.CostEstimate(
            flops=int(micros * 1.15e9), bytes_accessed=int(micros * 3.6e6), transcendentals=0
        ),
        name=kernel.__name__.removesuffix("_kernel"),
    )(*inputs, *far, *after)


def turn(values, cosine, sine):
    half = HEAD // 2
    swapped = jnp.concatenate([values[:, half:], values[:, :half]], axis=1)
    return values * cosine + swapped * sine


def back_kernel(index, segment, frequency, cotangent, out, cosine_out, sine_out):
    rows, length = cotangent.shape[0], segment.shape[1]
    base = index[0] * rows
    ids = segment[...]
    row = base + lax.broadcasted_iota(jnp.int32, (rows, length), 0)
    here = row == lax.broadcasted_iota(jnp.int32, (rows, length), 1)
    ids_wide = jnp.broadcast_to(ids, (rows, length)).astype(F32)
    own = jnp.sum(jnp.where(here, ids_wide, 0.0), axis=1, keepdims=True)
    first = jnp.sum(jnp.where(ids_wide < own, 1.0, 0.0), axis=1, keepdims=True)
    position = (row[:, :1]).astype(F32) - first
    angle = position * frequency[...]
    cosine = jnp.cos(angle)
    sign = jnp.where(
        lax.broadcasted_iota(jnp.int32, (rows, HEAD), 1) < HEAD // 2, -1.0, 1.0
    )
    sine = jnp.sin(angle) * sign
    cosine_out[...] = cosine
    sine_out[...] = sine
    heads = cotangent.shape[1] // HEAD
    for head in range(heads):
        value = cotangent[:, head * HEAD : (head + 1) * HEAD]
        if head < heads // 2:
            value = turn(value.astype(F32), cosine, -sine).astype(BF)
        out[:, head * HEAD : (head + 1) * HEAD] = value


def make_back(index, segment, frequency, cotangent):
    rows, columns = cotangent.shape
    return local_call(
        back_kernel,
        2,
        (index, segment, frequency, cotangent),
        [((rows, columns), BF, 1)] + [((rows, HEAD), F32, 1)] * 2,
    )


def tiles_kernel(slots, image, out, digits):
    width = out.shape[2]
    count = slots.shape[1]
    extra = out.shape[1] - image.shape[0]
    high = slots[...] >> 6
    digits[...] = jnp.zeros_like(digits)
    digits[:, :count] = high.astype(F32)
    digits[:, HEAD : HEAD + count] = (slots[...] - high * 64).astype(F32)
    first = lax.broadcasted_iota(jnp.int32, (extra, width), 0) == 0
    tail = jnp.where(first, digits[...], 0.0)
    for j in range(out.shape[0]):
        block = image[:, j * width : (j + 1) * width].astype(F32)
        out[j] = jnp.concatenate([block, tail], axis=0).astype(BF)


def make_tiles(image, slots, width):
    return local_call(
        tiles_kernel,
        2,
        (slots,),
        [((image.shape[1] // width, PAD, width), BF, 1)],
        (),
        (image,),
        [((1, width), F32)],
    )[0]


def hidden_kernel(place, slots, images, text, own, other, squares):
    count = slots.shape[1]
    rows = text.shape[0] // 8
    half = rows // 2
    core = place[8]
    line = lax.broadcasted_iota(jnp.int32, (rows, count), 0)
    for j in range(8):
        start = pl.multiple_of(place[j] * rows, rows)
        hit = (start + line == slots[...]).astype(F32)
        picked = jnp.dot(hit.astype(BF), images[...], preferred_element_type=F32)
        named = jnp.max(hit, axis=1, keepdims=True) > 0.5
        hidden = jnp.where(named, picked, text[pl.ds(start, rows), :].astype(F32))
        top, low = hidden[:half], hidden[half:]
        block = slice(j * half, (j + 1) * half)
        own[block] = jnp.where(core == 0, top, low).astype(BF)
        other[block] = jnp.where(core == 0, low, top).astype(BF)
        sums = jnp.concatenate([as_row(lanes(top * top)), as_row(lanes(low * low))], axis=1)
        for k in range(squares.shape[0]):
            squares[k, :, pl.ds(start, rows)] = sums


def build_hidden(place, slots, images, text, after):
    rows, width = text.shape
    return local_call(
        hidden_kernel,
        5,
        (place, slots),
        [((rows // 2, width), BF, 1)] * 2 + [((16, 1, rows), F32, 1)],
        after,
        (images, text),
    )


def lanes(values):
    total = values[:, :HEAD]
    for k in range(1, values.shape[1] // HEAD):
        total = total + values[:, k * HEAD : (k + 1) * HEAD]
    return total


def as_row(partial):
    return jnp.sum(partial.T, axis=0, keepdims=True)


def as_column(row):
    return jnp.broadcast_to(row, (HEAD, HEAD)).T


def part_of(place, j, rows):
    return pl.ds(pl.multiple_of(place[j] * rows, rows), rows)


def project_kernel(
    ready, done, gain_own, gain_met, own, met, weight_own, weight_met, *refs
):
    *out, scaled_own, scaled_met = refs
    rows = out[0].shape[0]
    columns = weight_own.shape[1]
    for copy in ready[:2]:
        copy.wait()
    scaled_own[...] = (own[...].astype(F32) * gain_own[...]).astype(BF)
    scaled_met[...] = (met[...].astype(F32) * gain_met[...]).astype(BF)
    for copy in ready[2:]:
        copy.wait()
    for j in range(0, 8, 4):
        block = slice(j * rows, (j + 4) * rows)
        for n in range(0, columns, 512):
            part = slice(n, n + 512)
            total = (
                jnp.dot(scaled_own[block], weight_own[:, part], preferred_element_type=F32)
                + jnp.dot(scaled_met[block], weight_met[:, part], preferred_element_type=F32)
            ).astype(BF)
            for k in range(4):
                out[j + k][:, part] = total[k * rows : (k + 1) * rows]
        for k in range(4):
            done[j + k].start()


def project(own, met, gain_own, gain_met, weight_own, weight_met):
    rows, width = own.shape
    columns = weight_own.shape[1]
    return local_call(
        project_kernel,
        60,
        (gain_own, gain_met),
        [((rows // 8, columns), BF, 1)] * 8,
        far=(own, met, weight_own, weight_met),
        scratch=[((rows, width), BF)] * 2,
        lazy=True,
    )


def normed_lines(source, scale, gain, out):
    rows = source.shape[0] // 8
    for j in range(8):
        block = slice(j * rows, (j + 1) * rows)
        wide = jnp.concatenate([scale[block]] * (source.shape[1] // HEAD), axis=1)
        out[:, block] = (source[block].astype(F32) * wide * gain[...]).astype(BF).T


def fill_weight_grad(normed, whole, out):
    width, columns = normed.shape[0], whole.shape[1]
    share = columns // 8
    for j in range(0, 8, 2):
        total = jnp.dot(
            normed[...], whole[:, j * share : (j + 2) * share], preferred_element_type=F32
        ).astype(BF)
        for k in range(2):
            out[j + k, :width, :] = total[:, k * share : (k + 1) * share]


def fill_extra(bias, gain, out):
    width, share = gain.shape[1], out.shape[2]
    line = lax.broadcasted_iota(jnp.int32, (16, share), 0)
    lines = jnp.zeros((16, share), F32)
    for k in range(width // HEAD):
        part = gain[:, k * HEAD : (k + 1) * HEAD]
        lines = jnp.where(line == k + 1, jnp.concatenate([part, part], axis=1), lines)
    for j in range(8):
        extra = jnp.where(line == 0, bias[:, j * share : (j + 1) * share], lines)
        out[j, width:, :] = extra.astype(BF)


def own_grads_kernel(ready, done, place, gain_own, gain_met, squares, own, *refs):
    back, terms, (met, weight_own, weight_met) = refs[:16:2], refs[1:16:2], refs[16:19]
    out, inner, scale, grad_own, grad_met, sum_met, whole, normed, sums, sum_own = refs[19:]
    rows, columns = back[0].shape
    core = place[8]
    sums[...] = gather_sum(squares)
    for j in range(8):
        start = pl.multiple_of((2 * place[j] + core) * rows, rows)
        total = sums[:, pl.ds(start, rows)]
        scale[j * rows : (j + 1) * rows] = as_column(lax.rsqrt(total / D + epsilon_value))
    done[2].start()
    ready[0].wait()
    normed_lines(own, scale, gain_own, normed)
    bias = jnp.zeros((1, columns), F32)
    for j in range(8):
        ready[2 * j + 1].wait()
        ready[2 * j + 2].wait()
        whole[j * rows : (j + 1) * rows] = back[j][...]
        value = back[j][...].astype(F32)
        bias += jnp.sum(value, axis=0, keepdims=True)
        line = as_row(lanes(value * terms[j][...].astype(F32)))
        start = pl.multiple_of(place[j] * rows, rows)
        for k in range(inner.shape[0]):
            inner[k, :, pl.ds(start, rows)] = line
    done[1].start()
    fill_weight_grad(normed, whole, out)
    for copy in ready[17:]:
        copy.wait()
    last = (((1,), (1,)), ((), ()))
    sum_own[...] = jnp.zeros_like(sum_own)
    sum_met[...] = jnp.zeros_like(sum_met)
    for source, gain, weight, grad, total, copy in (
        (met, gain_met, weight_met, grad_met, sum_met, done[4]),
        (own, gain_own, weight_own, grad_own, sum_own, done[3]),
    ):
        for j in range(0, 8, 4):
            block = slice(j * rows, (j + 4) * rows)
            s = jnp.concatenate([scale[block]] * 2, axis=1)
            for n in range(0, own.shape[1], 256):
                part = slice(n, n + 256)
                scaled = s * lax.dot_general(
                    whole[block], weight[part], last, preferred_element_type=F32
                )
                grad[block, part] = (scaled * gain[:, part]).astype(BF)
                total[:, part] += jnp.sum(
                    scaled * source[block, part].astype(F32), axis=0, keepdims=True
                )
        copy.start()
    fill_extra(bias, sum_own[...], out)
    done[0].start()


def own_grads(
    place, gain_own, gain_met, squares, own, met, weight_own, weight_met, back, terms
):
    rows, width = own.shape
    columns = back[0].shape[1]
    pieces = [value for pair in zip(back, terms) for value in pair]
    return local_call(
        own_grads_kernel,
        14,
        (place, gain_own, gain_met, squares),
        [
            ((8, width + 16, columns // 8), BF, 1),
            ((16, 1, rows), F32, 1),
            ((rows, HEAD), F32, 1),
            ((rows, width), BF, 1),
            ((rows, width), BF, 1),
            ((1, width), F32),
        ],
        (),
        (own, *pieces, met, weight_own, weight_met),
        [((rows, columns), BF), ((width, rows), BF), ((1, 2 * rows), F32), ((1, width), F32)],
        lazy=True,
    )


def met_grads_kernel(ready, done, gain, gain_sum, met, scale, *refs):
    back, (far_term, across_term, one, two, over) = refs[:8], refs[8:13]
    out, far, across, whole, normed = refs[13:]
    rows, columns = back[0].shape
    for copy in ready[:2]:
        copy.wait()
    normed_lines(met, scale, gain, normed)
    bias = jnp.zeros((1, columns), F32)
    for j in range(8):
        ready[j + 2].wait()
        value = back[j][...]
        whole[j * rows : (j + 1) * rows] = value
        bias += jnp.sum(value.astype(F32), axis=0, keepdims=True)
    fill_weight_grad(normed, whole, out)
    fill_extra(bias, gain_sum[...], out)
    done[0].start()
    for copy in ready[10:]:
        copy.wait()
    far[...] = add(far_term[...], over[...])
    done[1].start()
    across[...] = add(across_term[...], one[...], two[...])
    done[2].start()


def met_grads(gain, gain_sum, met, scale, back, terms, arrived):
    rows, width = met.shape
    columns = back[0].shape[1]
    return local_call(
        met_grads_kernel,
        6,
        (gain, gain_sum),
        [((8, width + 16, columns // 8), BF, 1)] + [((rows // 8, columns), BF, 1)] * 2,
        (),
        (met, scale, *back, *terms, *arrived),
        [((rows, columns), BF), ((width, rows), BF)],
        lazy=True,
    )


def split_kernel(
    place, slots, slot_lines, squares, inner,
    grad_own, grad_other, own, other, text, images, whole, pulls,
):
    count = slots.shape[1]
    core = place[8]
    half = own.shape[0] // 8
    rows = 2 * half
    width = own.shape[1]
    line = lax.broadcasted_iota(jnp.int32, (rows, count), 0)
    even, odd = inner[0], inner[1]
    for k in range(2, inner.shape[0], 2):
        even, odd = even + inner[k], odd + inner[k + 1]
    whole_inner = jnp.concatenate(
        [v[:, k * half : (k + 1) * half] for k in range(8) for v in (even, odd)], axis=1
    )
    scale = lax.rsqrt(gather_sum(squares) / D + epsilon_value)
    pull_row = scale * scale * scale * whole_inner / D
    pulls[...] = jnp.broadcast_to(pull_row, pulls.shape)
    for j in range(8):
        block = slice(j * half, (j + 1) * half)
        start = pl.multiple_of(place[j] * rows, rows)
        values = []
        for grad, hidden in ((grad_own, own), (grad_other, other)):
            values.append((grad[block].astype(F32), hidden[block].astype(F32)))
        (one, one_hidden), (two, two_hidden) = values
        value = jnp.concatenate(
            [jnp.where(core == 0, one, two), jnp.where(core == 0, two, one)], axis=0
        )
        hidden = jnp.concatenate(
            [
                jnp.where(core == 0, one_hidden, two_hidden),
                jnp.where(core == 0, two_hidden, one_hidden),
            ],
            axis=0,
        )
        near = pulls[:1, pl.ds(start, rows)]
        pull = jnp.concatenate([as_column(near[:, :half]), as_column(near[:, half:])], axis=0)
        value = value - hidden * jnp.concatenate([pull] * (width // HEAD), axis=1)
        hit = (start + line == slots[...]).astype(F32)
        named = jnp.max(hit, axis=1, keepdims=True) > 0.5
        whole[pl.ds(start, rows), :] = value.astype(BF)
        text[pl.ds(start, rows), :] = jnp.where(named, 0.0, value).astype(BF)
    tokens = whole.shape[0]
    for k in range(0, images.shape[0], 256):
        lines = slot_lines[k : k + 256]
        pick = (lax.broadcasted_iota(jnp.int32, (256, tokens), 1) == lines).astype(F32)
        images[k : k + 256] = jnp.dot(
            pick.astype(BF), whole[...], preferred_element_type=F32
        ).astype(BF)


def split_grads(
    place, slots, slot_lines, squares, inner, grad_own, grad_other, own, other, after,
):
    rows, width = own.shape
    count = slot_lines.shape[0]
    return local_call(
        split_kernel,
        5,
        (place, slots, slot_lines, squares, inner),
        [((2 * rows, width), BF, 1), ((count, width), BF, 1)],
        after,
        (grad_own, grad_other, own, other),
        [((2 * rows, width), BF), ((8, 2 * rows), F32)],
    )


def states_kernel(bias, here, left, right, far, across, scale, cosine, sine, out):
    c, s, factor = cosine[...], sine[...], scale[: out.shape[0]]
    heads = out.shape[1] // HEAD
    for head in range(heads):
        block = slice(head * HEAD, (head + 1) * HEAD)
        value = here[:, block].astype(F32)
        for term in (left, right, far, across):
            value += term[:, block].astype(F32)
        value = value * factor + bias[:, block]
        if head < heads // 2:
            value = turn(value, c, s)
        out[:, block] = value.astype(BF)


def make_states(terms, scale, bias, cosine, sine):
    return local_call(
        states_kernel, 3, (bias,), [(terms[0].shape, BF, 1)], (), (*terms, scale, cosine, sine)
    )[0]


def join_kernel(tiles, out):
    width = tiles.shape[2]
    for j in range(tiles.shape[0]):
        out[:, j * width : (j + 1) * width] = tiles[j]


def join_tiles(tiles, after):
    count, rows, width = tiles.shape
    return local_call(join_kernel, 2, (), [((rows, count * width), BF, 1)], after, (tiles,))[0]


def per_device(
    text_embeds, image_tokens, image_slots, segment_ids, norm_gain, kv_weight, kv_bias, kv_cotangent
):
    mp_index = lax.axis_index("mp")
    dp, phase = lax.axis_index("dp"), lax.axis_index("phase")
    index = mp_index.astype(jnp.int32)[None]
    core, column, line = mp_index % 2, (mp_index // 2) % 4, mp_index // 8
    place = [((line + dy) % 2) * 4 + (column + dx) % 4 for dy, dx in ORDER]
    place = jnp.stack(place + [core]).astype(jnp.int32)
    width = kv_weight.shape[0]
    count = image_slots.shape[1]

    frequency = rope_base ** (-(np.arange(HEAD // 2, dtype=np.float32) * np.float32(2.0)) / HEAD)
    frequency = np.concatenate([frequency, frequency]).astype(np.float32)[None, :]
    own_back, cosine, sine = make_back(
        index, segment_ids, jnp.asarray(frequency), kv_cotangent[0]
    )
    images = exchange(make_tiles(image_tokens[0], image_slots, width))

    back = gather_rows(own_back)

    weight_own = kv_weight
    weight_met = swap_core(weight_own)
    gain_own = norm_gain[None, :]
    gain_met = swap_core(gain_own)

    digits = images[:, count, :].astype(jnp.int32)
    found = digits[:, :count] * 64 + digits[:, HEAD : HEAD + count]
    slots = jnp.pad(found, ((0, 0), (0, PAD - count)), constant_values=-1).reshape(1, -1)

    own, other, squares = build_hidden(
        place, slots, images.reshape(-1, width), text_embeds[0], (back[1], back[2], back[4])
    )
    squares = exchange(squares)
    met = swap_core(other)
    terms = project(own, met, gain_own, gain_met, weight_own, weight_met)
    arrived, met_terms = reduce_rows(terms)
    mine, inner, scale, grad_own, grad_sent, gain_sum = own_grads(
        place, gain_own, gain_met, squares, own, met, weight_own, weight_met, back, terms
    )
    met_late, _ = lax.optimization_barrier((met, met_terms[1:]))
    sent, far, across = met_grads(
        gain_met, gain_sum, met_late, scale, back, terms[3:5], arrived
    )
    met_terms = (*met_terms, take(far, 0, 2), take(across, 1, 0))
    inner = exchange(inner)
    met_mine = swap_core(sent)
    states = make_states(met_terms, scale, kv_bias[None, :], cosine, sine)
    grad_other = swap_core(grad_sent)
    text_grad, image_rows = split_grads(
        place, slots, found.reshape(-1, 1), squares, inner,
        grad_own, grad_other, own, other, (),
    )
    image_tiles = exchange(image_rows.reshape(16, count, width))
    waits = {3: inner, 2: text_grad, 1: met_terms[3:], 0: (image_tiles, states)}
    sums = reduce_phases(phase, mine, met_mine, waits)
    kept = jnp.where(dp == 0, sums[:, :HEAD], sums[:, HEAD:])
    given = jnp.where(dp == 0, sums[:, HEAD:], sums[:, :HEAD]).astype(BF)
    parameter = kept + lax.ppermute(given, "dp", [(0, 1), (1, 0)]).astype(F32)
    weight_total = parameter[:width]
    bias_total = parameter[width]
    gain_total = parameter[width + 1 : width + 1 + width // HEAD].reshape(-1)
    image_grad = join_tiles(image_tiles, ())
    return (states[None], text_grad[None], image_grad[None], weight_total, bias_total, gain_total)


def solution(mesh):
    return jax.shard_map(
        per_device,
        mesh=mesh,
        in_specs=(
            P(("phase", "dp"), None, "mp"),
            P(("phase", "dp"), "mp", None),
            P(("phase", "dp"), "mp"),
            P(("phase", "dp"), None),
            P("mp"),
            P("mp", None),
            P(),
            P(("phase", "dp"), "mp", None),
        ),
        out_specs=(
            P(("phase", "dp"), "mp", None),
            P(("phase", "dp"), None, "mp"),
            P(("phase", "dp"), "mp", None),
            P("mp", ("phase", "dp")),
            P(("phase", "dp")),
            P("mp"),
        ),
        check_vma=False,
    )
```

```python
import jax
import jax.numpy as jnp
import numpy as np
from jax import lax
from jax.experimental import pallas as pl
from jax.experimental.pallas import tpu as pltpu
from jax.sharding import PartitionSpec as P

D = 8192
HEAD = 128
PAD = 56
epsilon_value = 1e-06
rope_base = 1000000.0

BF = jnp.bfloat16
F32 = jnp.float32
MIB = 1 << 20
HIGH = lax.Precision.HIGHEST

ORDER = ((0, 0), (0, 1), (0, 3), (0, 2), (1, 0), (1, 1), (1, 3), (1, 2))


def take(value, dy, dx, dc=0):
    pairs = []
    for y in range(2):
        for x in range(4):
            for c in range(2):
                source = (((y + dy) % 2) * 4 + (x + dx) % 4) * 2 + (c + dc) % 2
                pairs.append((source, (y * 4 + x) * 2 + c))
    return lax.ppermute(value, "mp", pairs)


def swap_core(value):
    return take(value, 0, 0, 1)


def exchange(value):
    return lax.all_to_all(value, "mp", split_axis=0, concat_axis=0, tiled=True)


def spread(row, out):
    for k in range(out.shape[0]):
        out[k] = row


def gather_sum(terms):
    total = terms[0]
    for k in range(1, terms.shape[0]):
        total = total + terms[k]
    return total


def gather_rows(block):
    right, left, far = take(block, 0, 1), take(block, 0, 3), take(block, 0, 2)
    across = take(block, 1, 0)
    return [
        block, right, left, far,
        across, take(across, 0, 1), take(across, 0, 3), take(far, 1, 0),
    ]


def add(*values):
    total = values[0].astype(F32)
    for value in values[1:]:
        total = total + value.astype(F32)
    return total.astype(BF)


def reduce_rows(terms):
    here, right, left, far, across, across_right, across_left, across_far = terms
    one, two = take(across_right, 0, 3), take(across_left, 0, 1)
    over = take(across_far, 1, 0)
    return (one, two, over), (here, take(right, 0, 3), take(left, 0, 1))


def take_phase(value, dz):
    return lax.ppermute(value, "phase", [((p + dz) % 8, p) for p in range(8)])


def reduce_phases(phase, mine, met, waits):
    def block(dz, *arrived):
        at = lax.rem(phase + dz, 8)
        own = lax.dynamic_index_in_dim(mine, at, 0, False).astype(F32)
        other = lax.dynamic_index_in_dim(met, at, 0, False).astype(F32)
        total = own + other
        for value in arrived:
            total = total + value.astype(F32)
        return total

    half = mine.shape[1] // 32 * 16
    rows = mine.shape[1]
    far = block(4).astype(BF)
    up = jnp.pad(take_phase(far[:half], -1), ((0, rows - half), (0, 0)))
    down = jnp.pad(take_phase(far[half:], 1), ((half, 0), (0, 0)))
    for step in (3, 2, 1):
        up, down, _ = lax.optimization_barrier((up, down, waits[step]))
        up = take_phase(block(step, up).astype(BF), -1)
        down = take_phase(block(8 - step, down).astype(BF), 1)
    up, down, _ = lax.optimization_barrier((up, down, waits[0]))
    return block(0, up, down)


def local_call(kernel, micros, inputs, out_shape, after=(), far=(), scratch=(), lazy=False):
    near, distant, extra = len(inputs), len(far), len(after)
    outs = len(out_shape)
    results = [k for k, entry in enumerate(out_shape) if len(entry) > 2]

    def body(*refs):
        given, held = list(refs[:near]), refs[near : near + distant]
        refs = refs[near + distant + extra :]
        out, refs = list(refs[:outs]), refs[outs:]
        stages, refs = refs[:distant], refs[distant:]
        homes, refs = refs[: len(results)], refs[len(results) :]
        copies = [
            pltpu.make_async_copy(source, stage, refs[-1].at[k])
            for k, (source, stage) in enumerate(zip(held, stages))
        ]
        for copy in copies:
            copy.start()
        if not lazy:
            for copy in copies:
                copy.wait()
        targets = [out[k] for k in results]
        for k, home in zip(results, homes):
            out[k] = home
        back = [
            pltpu.make_async_copy(home, target, refs[-1].at[distant + k])
            for k, (home, target) in enumerate(zip(homes, targets))
        ]
        used = refs[:-1] if distant or results else refs
        if lazy:
            kernel(copies, back, *given, *stages, *out, *used)
        else:
            kernel(*given, *stages, *out, *used)
            for copy in back:
                copy.start()
        for copy in back:
            copy.wait()

    vmem = pl.BlockSpec(memory_space=pltpu.VMEM)
    smem = pl.BlockSpec(memory_space=pltpu.SMEM)
    hbm = pl.BlockSpec(memory_space=pltpu.HBM)
    staging = [pltpu.VMEM(value.shape, value.dtype) for value in far]
    staging += [pltpu.VMEM(*out_shape[k][:2]) for k in results]
    staging += [pltpu.VMEM(*entry) for entry in scratch]
    if distant or results:
        staging.append(pltpu.SemaphoreType.DMA((distant + len(results),)))
    return pl.pallas_call(
        body,
        in_specs=[smem if value.ndim == 1 else vmem for value in inputs] + [hbm] * (distant + extra),
        out_specs=[hbm if len(entry) > 2 else vmem for entry in out_shape],
        out_shape=[jax.ShapeDtypeStruct(*entry[:2]) for entry in out_shape],
        scratch_shapes=staging,
        compiler_params=pltpu.CompilerParams(vmem_limit_bytes=60 * MIB),
        cost_estimate=pl.CostEstimate(
            flops=int(micros * 1.15e9), bytes_accessed=int(micros * 3.6e6), transcendentals=0
        ),
        name=kernel.__name__.removesuffix("_kernel"),
    )(*inputs, *far, *after)


def turn(values, cosine, sine):
    half = HEAD // 2
    swapped = jnp.concatenate([values[:, half:], values[:, :half]], axis=1)
    return values * cosine + swapped * sine


def back_kernel(index, segment, frequency, cotangent, out, cosine_out, sine_out):
    rows, length = cotangent.shape[0], segment.shape[1]
    base = index[0] * rows
    ids = segment[...]
    row = base + lax.broadcasted_iota(jnp.int32, (rows, length), 0)
    here = row == lax.broadcasted_iota(jnp.int32, (rows, length), 1)
    ids_wide = jnp.broadcast_to(ids, (rows, length)).astype(F32)
    own = jnp.sum(jnp.where(here, ids_wide, 0.0), axis=1, keepdims=True)
    first = jnp.sum(jnp.where(ids_wide < own, 1.0, 0.0), axis=1, keepdims=True)
    position = (row[:, :1]).astype(F32) - first
    angle = position * frequency[...]
    cosine = jnp.cos(angle)
    sign = jnp.where(
        lax.broadcasted_iota(jnp.int32, (rows, HEAD), 1) < HEAD // 2, -1.0, 1.0
    )
    sine = jnp.sin(angle) * sign
    cosine_out[...] = cosine
    sine_out[...] = sine
    heads = cotangent.shape[1] // HEAD
    for head in range(heads):
        value = cotangent[:, head * HEAD : (head + 1) * HEAD]
        if head < heads // 2:
            value = turn(value.astype(F32), cosine, -sine).astype(BF)
        out[:, head * HEAD : (head + 1) * HEAD] = value


def make_back(index, segment, frequency, cotangent):
    rows, columns = cotangent.shape
    return local_call(
        back_kernel,
        2,
        (index, segment, frequency, cotangent),
        [((rows, columns), BF, 1)] + [((rows, HEAD), F32, 1)] * 2,
    )


def tiles_kernel(slots, image, out, digits):
    width = out.shape[2]
    count = slots.shape[1]
    extra = out.shape[1] - image.shape[0]
    high = slots[...] >> 6
    digits[...] = jnp.zeros_like(digits)
    digits[:, :count] = high.astype(F32)
    digits[:, HEAD : HEAD + count] = (slots[...] - high * 64).astype(F32)
    first = lax.broadcasted_iota(jnp.int32, (extra, width), 0) == 0
    tail = jnp.where(first, digits[...], 0.0)
    for j in range(out.shape[0]):
        block = image[:, j * width : (j + 1) * width].astype(F32)
        out[j] = jnp.concatenate([block, tail], axis=0).astype(BF)


def make_tiles(image, slots, width):
    return local_call(
        tiles_kernel,
        2,
        (slots,),
        [((image.shape[1] // width, PAD, width), BF, 1)],
        (),
        (image,),
        [((1, width), F32)],
    )[0]


def hidden_kernel(place, slots, images, text, own, other, squares):
    count = slots.shape[1]
    rows = text.shape[0] // 8
    half = rows // 2
    core = place[8]
    line = lax.broadcasted_iota(jnp.int32, (rows, count), 0)
    for j in range(8):
        start = pl.multiple_of(place[j] * rows, rows)
        hit = (start + line == slots[...]).astype(F32)
        picked = jnp.dot(hit.astype(BF), images[...], preferred_element_type=F32)
        named = jnp.max(hit, axis=1, keepdims=True) > 0.5
        hidden = jnp.where(named, picked, text[pl.ds(start, rows), :].astype(F32))
        top, low = hidden[:half], hidden[half:]
        block = slice(j * half, (j + 1) * half)
        own[block] = jnp.where(core == 0, top, low).astype(BF)
        other[block] = jnp.where(core == 0, low, top).astype(BF)
        sums = jnp.concatenate([as_row(lanes(top * top)), as_row(lanes(low * low))], axis=1)
        for k in range(squares.shape[0]):
            squares[k, :, pl.ds(start, rows)] = sums


def build_hidden(place, slots, images, text, after):
    rows, width = text.shape
    return local_call(
        hidden_kernel,
        5,
        (place, slots),
        [((rows // 2, width), BF, 1)] * 2 + [((16, 1, rows), F32, 1)],
        after,
        (images, text),
    )


def lanes(values):
    total = values[:, :HEAD]
    for k in range(1, values.shape[1] // HEAD):
        total = total + values[:, k * HEAD : (k + 1) * HEAD]
    return total


def as_row(partial):
    return jnp.sum(partial.T, axis=0, keepdims=True)


def as_column(row):
    return jnp.broadcast_to(row, (HEAD, HEAD)).T


def part_of(place, j, rows):
    return pl.ds(pl.multiple_of(place[j] * rows, rows), rows)


def project_kernel(
    ready, done, gain_own, gain_met, own, met, weight_own, weight_met, *refs
):
    *out, scaled_own, scaled_met = refs
    rows = out[0].shape[0]
    columns = weight_own.shape[1]
    for copy in ready[:2]:
        copy.wait()
    scaled_own[...] = (own[...].astype(F32) * gain_own[...]).astype(BF)
    scaled_met[...] = (met[...].astype(F32) * gain_met[...]).astype(BF)
    for copy in ready[2:]:
        copy.wait()
    for j in range(0, 8, 4):
        block = slice(j * rows, (j + 4) * rows)
        for n in range(0, columns, 512):
            part = slice(n, n + 512)
            total = (
                jnp.dot(scaled_own[block], weight_own[:, part], preferred_element_type=F32)
                + jnp.dot(scaled_met[block], weight_met[:, part], preferred_element_type=F32)
            ).astype(BF)
            for k in range(4):
                out[j + k][:, part] = total[k * rows : (k + 1) * rows]
        for k in range(4):
            done[j + k].start()


def project(own, met, gain_own, gain_met, weight_own, weight_met):
    rows, width = own.shape
    columns = weight_own.shape[1]
    return local_call(
        project_kernel,
        60,
        (gain_own, gain_met),
        [((rows // 8, columns), BF, 1)] * 8,
        far=(own, met, weight_own, weight_met),
        scratch=[((rows, width), BF)] * 2,
        lazy=True,
    )


def normed_lines(source, scale, gain, out):
    rows = source.shape[0] // 8
    for j in range(8):
        block = slice(j * rows, (j + 1) * rows)
        wide = jnp.concatenate([scale[block]] * (source.shape[1] // HEAD), axis=1)
        out[:, block] = (source[block].astype(F32) * wide * gain[...]).astype(BF).T


def fill_weight_grad(normed, whole, out):
    width, columns = normed.shape[0], whole.shape[1]
    share = columns // 8
    for j in range(0, 8, 2):
        total = jnp.dot(
            normed[...], whole[:, j * share : (j + 2) * share], preferred_element_type=F32
        ).astype(BF)
        for k in range(2):
            out[j + k, :width, :] = total[:, k * share : (k + 1) * share]


def fill_extra(bias, gain, out):
    width, share = gain.shape[1], out.shape[2]
    line = lax.broadcasted_iota(jnp.int32, (16, share), 0)
    lines = jnp.zeros((16, share), F32)
    for k in range(width // HEAD):
        part = gain[:, k * HEAD : (k + 1) * HEAD]
        lines = jnp.where(line == k + 1, jnp.concatenate([part, part], axis=1), lines)
    for j in range(8):
        extra = jnp.where(line == 0, bias[:, j * share : (j + 1) * share], lines)
        out[j, width:, :] = extra.astype(BF)


def own_grads_kernel(ready, done, place, gain_own, gain_met, squares, own, *refs):
    back, terms, (met, weight_own, weight_met) = refs[:16:2], refs[1:16:2], refs[16:19]
    out, inner, scale, grad_own, grad_met, sum_met, whole, normed, sums, sum_own = refs[19:]
    rows, columns = back[0].shape
    core = place[8]
    sums[...] = gather_sum(squares)
    for j in range(8):
        start = pl.multiple_of((2 * place[j] + core) * rows, rows)
        total = sums[:, pl.ds(start, rows)]
        scale[j * rows : (j + 1) * rows] = as_column(lax.rsqrt(total / D + epsilon_value))
    done[2].start()
    ready[0].wait()
    normed_lines(own, scale, gain_own, normed)
    bias = jnp.zeros((1, columns), F32)
    for j in range(8):
        ready[2 * j + 1].wait()
        ready[2 * j + 2].wait()
        whole[j * rows : (j + 1) * rows] = back[j][...]
        value = back[j][...].astype(F32)
        bias += jnp.sum(value, axis=0, keepdims=True)
        line = as_row(lanes(value * terms[j][...].astype(F32)))
        start = pl.multiple_of(place[j] * rows, rows)
        for k in range(inner.shape[0]):
            inner[k, :, pl.ds(start, rows)] = line
    done[1].start()
    fill_weight_grad(normed, whole, out)
    for copy in ready[17:]:
        copy.wait()
    last = (((1,), (1,)), ((), ()))
    sum_own[...] = jnp.zeros_like(sum_own)
    sum_met[...] = jnp.zeros_like(sum_met)
    for source, gain, weight, grad, total, copy in (
        (met, gain_met, weight_met, grad_met, sum_met, done[4]),
        (own, gain_own, weight_own, grad_own, sum_own, done[3]),
    ):
        for j in range(0, 8, 4):
            block = slice(j * rows, (j + 4) * rows)
            s = jnp.concatenate([scale[block]] * 2, axis=1)
            for n in range(0, own.shape[1], 256):
                part = slice(n, n + 256)
                scaled = s * lax.dot_general(
                    whole[block], weight[part], last, preferred_element_type=F32
                )
                grad[block, part] = (scaled * gain[:, part]).astype(BF)
                total[:, part] += jnp.sum(
                    scaled * source[block, part].astype(F32), axis=0, keepdims=True
                )
        copy.start()
    fill_extra(bias, sum_own[...], out)
    done[0].start()


def own_grads(
    place, gain_own, gain_met, squares, own, met, weight_own, weight_met, back, terms
):
    rows, width = own.shape
    columns = back[0].shape[1]
    pieces = [value for pair in zip(back, terms) for value in pair]
    return local_call(
        own_grads_kernel,
        14,
        (place, gain_own, gain_met, squares),
        [
            ((8, width + 16, columns // 8), BF, 1),
            ((16, 1, rows), F32, 1),
            ((rows, HEAD), F32, 1),
            ((rows, width), BF, 1),
            ((rows, width), BF, 1),
            ((1, width), F32),
        ],
        (),
        (own, *pieces, met, weight_own, weight_met),
        [((rows, columns), BF), ((width, rows), BF), ((1, 2 * rows), F32), ((1, width), F32)],
        lazy=True,
    )


def met_grads_kernel(ready, done, gain, gain_sum, met, scale, *refs):
    back, (far_term, across_term, one, two, over) = refs[:8], refs[8:13]
    out, far, across, whole, normed = refs[13:]
    rows, columns = back[0].shape
    for copy in ready[:2]:
        copy.wait()
    normed_lines(met, scale, gain, normed)
    bias = jnp.zeros((1, columns), F32)
    for j in range(8):
        ready[j + 2].wait()
        value = back[j][...]
        whole[j * rows : (j + 1) * rows] = value
        bias += jnp.sum(value.astype(F32), axis=0, keepdims=True)
    fill_weight_grad(normed, whole, out)
    fill_extra(bias, gain_sum[...], out)
    done[0].start()
    for copy in ready[10:]:
        copy.wait()
    far[...] = add(far_term[...], over[...])
    done[1].start()
    across[...] = add(across_term[...], one[...], two[...])
    done[2].start()


def met_grads(gain, gain_sum, met, scale, back, terms, arrived):
    rows, width = met.shape
    columns = back[0].shape[1]
    return local_call(
        met_grads_kernel,
        6,
        (gain, gain_sum),
        [((8, width + 16, columns // 8), BF, 1)] + [((rows // 8, columns), BF, 1)] * 2,
        (),
        (met, scale, *back, *terms, *arrived),
        [((rows, columns), BF), ((width, rows), BF)],
        lazy=True,
    )


def split_kernel(
    place, slots, slot_lines, squares, inner,
    grad_own, grad_other, own, other, text, images, whole, pulls,
):
    count = slots.shape[1]
    core = place[8]
    half = own.shape[0] // 8
    rows = 2 * half
    width = own.shape[1]
    line = lax.broadcasted_iota(jnp.int32, (rows, count), 0)
    even, odd = inner[0], inner[1]
    for k in range(2, inner.shape[0], 2):
        even, odd = even + inner[k], odd + inner[k + 1]
    whole_inner = jnp.concatenate(
        [v[:, k * half : (k + 1) * half] for k in range(8) for v in (even, odd)], axis=1
    )
    scale = lax.rsqrt(gather_sum(squares) / D + epsilon_value)
    pull_row = scale * scale * scale * whole_inner / D
    pulls[...] = jnp.broadcast_to(pull_row, pulls.shape)
    for j in range(8):
        block = slice(j * half, (j + 1) * half)
        start = pl.multiple_of(place[j] * rows, rows)
        values = []
        for grad, hidden in ((grad_own, own), (grad_other, other)):
            values.append((grad[block].astype(F32), hidden[block].astype(F32)))
        (one, one_hidden), (two, two_hidden) = values
        value = jnp.concatenate(
            [jnp.where(core == 0, one, two), jnp.where(core == 0, two, one)], axis=0
        )
        hidden = jnp.concatenate(
            [
                jnp.where(core == 0, one_hidden, two_hidden),
                jnp.where(core == 0, two_hidden, one_hidden),
            ],
            axis=0,
        )
        near = pulls[:1, pl.ds(start, rows)]
        pull = jnp.concatenate([as_column(near[:, :half]), as_column(near[:, half:])], axis=0)
        value = value - hidden * jnp.concatenate([pull] * (width // HEAD), axis=1)
        hit = (start + line == slots[...]).astype(F32)
        named = jnp.max(hit, axis=1, keepdims=True) > 0.5
        whole[pl.ds(start, rows), :] = value.astype(BF)
        text[pl.ds(start, rows), :] = jnp.where(named, 0.0, value).astype(BF)
    tokens = whole.shape[0]
    for k in range(0, images.shape[0], 256):
        lines = slot_lines[k : k + 256]
        pick = (lax.broadcasted_iota(jnp.int32, (256, tokens), 1) == lines).astype(F32)
        images[k : k + 256] = jnp.dot(
            pick.astype(BF), whole[...], preferred_element_type=F32
        ).astype(BF)


def split_grads(
    place, slots, slot_lines, squares, inner, grad_own, grad_other, own, other, after,
):
    rows, width = own.shape
    count = slot_lines.shape[0]
    return local_call(
        split_kernel,
        5,
        (place, slots, slot_lines, squares, inner),
        [((2 * rows, width), BF, 1), ((count, width), BF, 1)],
        after,
        (grad_own, grad_other, own, other),
        [((2 * rows, width), BF), ((8, 2 * rows), F32)],
    )


def states_kernel(bias, here, left, right, far, across, scale, cosine, sine, out):
    c, s, factor = cosine[...], sine[...], scale[: out.shape[0]]
    heads = out.shape[1] // HEAD
    for head in range(heads):
        block = slice(head * HEAD, (head + 1) * HEAD)
        value = here[:, block].astype(F32)
        for term in (left, right, far, across):
            value += term[:, block].astype(F32)
        value = value * factor + bias[:, block]
        if head < heads // 2:
            value = turn(value, c, s)
        out[:, block] = value.astype(BF)


def make_states(terms, scale, bias, cosine, sine):
    return local_call(
        states_kernel, 3, (bias,), [(terms[0].shape, BF, 1)], (), (*terms, scale, cosine, sine)
    )[0]


def join_kernel(tiles, out):
    width = tiles.shape[2]
    for j in range(tiles.shape[0]):
        out[:, j * width : (j + 1) * width] = tiles[j]


def join_tiles(tiles, after):
    count, rows, width = tiles.shape
    return local_call(join_kernel, 2, (), [((rows, count * width), BF, 1)], after, (tiles,))[0]


def per_device(
    text_embeds, image_tokens, image_slots, segment_ids, norm_gain, kv_weight, kv_bias, kv_cotangent
):
    mp_index = lax.axis_index("mp")
    dp, phase = lax.axis_index("dp"), lax.axis_index("phase")
    index = mp_index.astype(jnp.int32)[None]
    core, column, line = mp_index % 2, (mp_index // 2) % 4, mp_index // 8
    place = [((line + dy) % 2) * 4 + (column + dx) % 4 for dy, dx in ORDER]
    place = jnp.stack(place + [core]).astype(jnp.int32)
    width = kv_weight.shape[0]
    count = image_slots.shape[1]

    frequency = rope_base ** (-(np.arange(HEAD // 2, dtype=np.float32) * np.float32(2.0)) / HEAD)
    frequency = np.concatenate([frequency, frequency]).astype(np.float32)[None, :]
    own_back, cosine, sine = make_back(
        index, segment_ids, jnp.asarray(frequency), kv_cotangent[0]
    )
    images = exchange(make_tiles(image_tokens[0], image_slots, width))

    back = gather_rows(own_back)

    weight_own = kv_weight
    weight_met = swap_core(weight_own)
    gain_own = norm_gain[None, :]
    gain_met = swap_core(gain_own)

    digits = images[:, count, :].astype(jnp.int32)
    found = digits[:, :count] * 64 + digits[:, HEAD : HEAD + count]
    slots = jnp.pad(found, ((0, 0), (0, PAD - count)), constant_values=-1).reshape(1, -1)

    own, other, squares = build_hidden(
        place, slots, images.reshape(-1, width), text_embeds[0], (back[1], back[2], back[4])
    )
    squares = exchange(squares)
    met = swap_core(other)
    terms = project(own, met, gain_own, gain_met, weight_own, weight_met)
    arrived, met_terms = reduce_rows(terms)
    mine, inner, scale, grad_own, grad_sent, gain_sum = own_grads(
        place, gain_own, gain_met, squares, own, met, weight_own, weight_met, back, terms
    )
    met_late, _ = lax.optimization_barrier((met, met_terms[1:]))
    sent, far, across = met_grads(
        gain_met, gain_sum, met_late, scale, back, terms[3:5], arrived
    )
    met_terms = (*met_terms, take(far, 0, 2), take(across, 1, 0))
    inner = exchange(inner)
    met_mine = swap_core(sent)
    states = make_states(met_terms, scale, kv_bias[None, :], cosine, sine)
    grad_other = swap_core(grad_sent)
    text_grad, image_rows = split_grads(
        place, slots, found.reshape(-1, 1), squares, inner,
        grad_own, grad_other, own, other, (),
    )
    image_tiles = exchange(image_rows.reshape(16, count, width))
    waits = {3: (inner, *met_terms[3:]), 2: text_grad, 1: scale, 0: (image_tiles, states)}
    sums = reduce_phases(phase, mine, met_mine, waits)
    kept = jnp.where(dp == 0, sums[:, :HEAD], sums[:, HEAD:])
    given = jnp.where(dp == 0, sums[:, HEAD:], sums[:, :HEAD]).astype(BF)
    parameter = kept + lax.ppermute(given, "dp", [(0, 1), (1, 0)]).astype(F32)
    weight_total = parameter[:width]
    bias_total = parameter[width]
    gain_total = parameter[width + 1 : width + 1 + width // HEAD].reshape(-1)
    image_grad = join_tiles(image_tiles, ())
    return (states[None], text_grad[None], image_grad[None], weight_total, bias_total, gain_total)


def solution(mesh):
    return jax.shard_map(
        per_device,
        mesh=mesh,
        in_specs=(
            P(("phase", "dp"), None, "mp"),
            P(("phase", "dp"), "mp", None),
            P(("phase", "dp"), "mp"),
            P(("phase", "dp"), None),
            P("mp"),
            P("mp", None),
            P(),
            P(("phase", "dp"), "mp", None),
        ),
        out_specs=(
            P(("phase", "dp"), "mp", None),
            P(("phase", "dp"), None, "mp"),
            P(("phase", "dp"), "mp", None),
            P("mp", ("phase", "dp")),
            P(("phase", "dp")),
            P("mp"),
        ),
        check_vma=False,
    )
```
